32 devices in a mesh: grp: 2 (over y), sta: 4 (over z), tm: 2 (over x), comp: 2 (over core).
Axes of the slice: x: 2, y: 2, z: 4, core: 2. Of those that a mesh axis runs over, the one named last changes fastest.
Arguments:
- data: bfloat16 [16, 3, 4096], P(('grp', 'sta'), None, 'tm'), parts along dimension 0, may hold values from -240 to 240
- templates: bfloat16 [16, 64, 3, 400], P(('grp', 'sta'), 'comp'), parts along dimension 0, may hold values from -6 to 6
- moveouts: int32 [16, 64], P(('grp', 'sta'), 'comp'), parts along dimension 0, may hold values from 0 to 624, as said below
- mask: int32 [16, 4], P(('grp', 'sta'), 'tm'), parts along dimension 0, may hold values from 0 to 1, as said below
Outputs:
- network: float32 [128, 4096], P(('grp', 'comp'), 'tm'), parts along dimension 0
The draws below stay inside these ranges and needn't reach their ends.
There are 2 independent parts, one for each index of `grp`. The reference program is written for one: setup_inputs(seed, part) draws one part's arguments, and reference() takes and returns one part's arrays. A program takes and returns all parts, laid end to end along the dimension named above; each array names one. Nothing has to cross between parts.
Inputs may be any that keep to these rules, and one draw needn't show every extreme that they name: `moveouts`: for every template some station has shift 625 - 1 and some station has shift 0. `mask`: every availability block has at least one available station.
All inputs are finite; a program needn't handle non-finite values.
Results may differ from the reference program's by a relative error of at most 0.0003.
Values may be sent and summed in bfloat16 or wider, within the bound.
No kernel may reach another device: no remote copies, remote signals or barrier semaphores. Data moves between devices by JAX's collectives and lax.ppermute only.
A program may use at most 64 MiB of HBM per device.

```python
import math
import jax
import jax.numpy as jnp
from jax import lax

NT = 64
L = 400
MOVE = 625
BLK = 1024
S = 8
STRETCHES = 4
TIME = 4096


def draw_data(key, part):
    key = jax.random.fold_in(key, 11)
    first, second, third = jax.random.split(key, 3)
    station = jnp.exp(jax.random.uniform(first, (S, 1, 1), minval=0.0, maxval=math.log(10.0)))
    envelope = jnp.exp(jax.random.uniform(second, (S, 1, TIME // 16, 1), minval=0.0, maxval=math.log(4.0)))
    envelope = jnp.broadcast_to(envelope, (S, 1, TIME // 16, 16)).reshape(S, 1, TIME)
    base = jnp.clip(jax.random.normal(third, (S, 3, TIME)), -6.0, 6.0)
    return (base * station * envelope).astype(jnp.bfloat16)


def draw_moveouts(key, part):
    key = jax.random.fold_in(key, 23)
    first, second, third = jax.random.split(key, 3)
    shifts = jax.random.randint(first, (S, NT), 0, MOVE)
    highest = jax.random.randint(second, (1, NT), 0, S)
    lowest = jax.random.randint(third, (1, NT), 0, S)
    lowest = jnp.where(lowest == highest, (lowest + 1) % S, lowest)
    stations = jnp.arange(S)[:, None]
    shifts = jnp.where(stations == highest, MOVE - 1, shifts)
    shifts = jnp.where(stations == lowest, 0, shifts)
    return shifts.astype(jnp.int32)


def draw_mask(key, part):
    key = jax.random.fold_in(key, 37)
    first, second = jax.random.split(key, 2)
    stations = jnp.arange(S)[:, None]
    percent = 25 + 60 * stations // max(S - 1, 1)
    flags = (jax.random.randint(first, (S, STRETCHES), 0, 100) < percent).astype(jnp.int32)
    forced = jax.random.randint(second, (1, STRETCHES), 0, S)
    flags = jnp.where(stations == forced, 1, flags)
    return flags.astype(jnp.int32)


def steps_of(own_key, extent, shards, smallest, top_value):
    def one(dim, blocks):
        draws = jax.random.uniform(jax.random.fold_in(jax.random.fold_in(own_key, 6), dim), (blocks,), jnp.float32, smallest / len(shards), top_value / len(shards))
        return jnp.repeat(jnp.exp(draws), extent[dim] // blocks).reshape((-1,) + (1,) * (len(extent) - dim - 1))

    level = one(*shards[0])
    for cut in shards[1:]:
        level = level * one(*cut)
    return level


def scatter_about(key, shape, deviation, bound, pieces=(), kind=jnp.bfloat16):
    entries = deviation * jax.random.normal(key, shape, jnp.float32)
    if pieces:
        entries = entries * steps_of(key, shape, pieces, -0.22, 0.18)
    return jnp.clip(entries, -bound, bound).astype(kind)


def setup_inputs(seed: int = 0, part: int = 0) -> dict:
    seeds = jax.random.split(jax.random.key(seed), 5)
    own_keys = jax.random.split(jax.random.fold_in(seeds[4], part), 5)
    data = draw_data(jax.random.fold_in(jax.random.fold_in(seeds[4], part), 71), part)
    templates = scatter_about(own_keys[1], (S, NT, 3, L), 1.0, 6.0, ((0, 4), (1, 2)))
    moveouts = draw_moveouts(jax.random.fold_in(jax.random.fold_in(seeds[4], part), 71), part)
    mask = draw_mask(jax.random.fold_in(jax.random.fold_in(seeds[4], part), 71), part)
    return dict(data=data, templates=templates, moveouts=moveouts, mask=mask)


eps_energy = 1e-06

def station_term(totals, inputs):
    waveform, bank, shifts, flags = inputs
    signal = waveform.astype(jnp.float32)
    filters = bank.astype(jnp.float32)
    products = lax.conv_general_dilated(signal[None], filters, (1,), 'VALID', dimension_numbers=('NCH', 'OIH', 'NCH'), precision=lax.Precision.HIGHEST)[0]
    squares = lax.optimization_barrier(jnp.sum(signal * signal, axis=0))
    boxcar = jnp.ones((1, 1, L), jnp.float32)
    energy = lax.conv_general_dilated(squares[None, None], boxcar, (1,), 'VALID', dimension_numbers=('NCH', 'OIH', 'NCH'), precision=lax.Precision.HIGHEST)[0, 0]
    template_scale = lax.rsqrt(lax.optimization_barrier(jnp.sum(filters * filters, axis=(1, 2))) + eps_energy)
    normalized = jnp.where(energy[None, :] > 0.0, products * template_scale[:, None] * lax.rsqrt(energy + eps_energy)[None, :], 0.0)
    positions = shifts.astype(jnp.int32)[:, None] + jnp.arange(TIME, dtype=jnp.int32)[None, :]
    aligned = jnp.take_along_axis(normalized, positions, axis=1)
    weight = jnp.repeat(flags.astype(jnp.float32), BLK)
    return ((totals[0] + weight[None, :] * aligned, totals[1] + weight), None)

def reference(data, templates, moveouts, mask):
    padded = jnp.pad(data, ((0, 0), (0, 0), (0, L + MOVE - 1)))
    start = (jnp.zeros((NT, TIME), jnp.float32), jnp.zeros((TIME,), jnp.float32))
    (totals, counts), _ = lax.scan(station_term, start, (padded, templates, moveouts, mask))
    return totals * (math.sqrt(3.0 * L) * lax.rsqrt(counts))[None, :]
```

```python
import functools
import math

import jax
import jax.numpy as jnp
from jax import lax
from jax.experimental import pallas as pl
from jax.experimental.pallas import tpu as pltpu
from jax.sharding import PartitionSpec as P

MOVE = 625

eps_energy = 1e-06
LANES = 128
WIRE_SCALE = 2.0**13


def shifted(value, axis, steps):
    count = lax.axis_size(axis)
    first, last = (max(0, -steps), min(count, count - steps))
    return lax.ppermute(value, axis, [(source, source + steps) for source in range(first, last)])


def correlate(moves, flags, wave_ref, bank_ref, out_ref, hankel, aligned, sums, *, sizes):
    stations, comps, taps, count, samples, block_len = sizes
    width = wave_ref.shape[2]
    whole = taps // LANES
    tail = taps - whole * LANES
    lag = tail - 1
    span = -(-(samples + MOVE - 1) // LANES) * LANES
    rows = samples // LANES
    pitch = aligned.shape[0] // (stations * count)
    block_rows = block_len // LANES

    for s in range(stations):
        for c in range(comps):
            line = wave_ref[s, c : c + 1, :]
            base = jnp.broadcast_to(line, (16, width))
            for g in range(LANES // 16):
                amount = (16 * g - lag) % width
                hankel[(s * comps + c) * LANES + 16 * g : (s * comps + c) * LANES + 16 * g + 16, :] = pltpu.roll(
                    base, amount, 1, stride=1, stride_axis=0
                )

    for s in range(stations):
        wide = wave_ref[s].astype(jnp.float32)
        square = jnp.sum(wide * wide, axis=0, keepdims=True)
        windows = {1: square}
        step = 1
        while 2 * step <= taps:
            windows[2 * step] = windows[step] + pltpu.roll(windows[step], width - step, 1)
            step *= 2
        energy, start = None, 0
        for size in sorted(windows, reverse=True):
            if start + size <= taps:
                piece = windows[size]
                piece = piece if start == 0 else pltpu.roll(piece, width - start, 1)
                energy = piece if energy is None else energy + piece
                start += size
        inverse = jnp.where(energy > 0.0, lax.rsqrt(energy + eps_energy), 0.0)
        bank = bank_ref[s]
        wide_bank = bank.astype(jnp.float32)
        scale = lax.rsqrt(jnp.sum(wide_bank * wide_bank, axis=1, keepdims=True) + eps_energy)
        for first in range(0, span, 256):
            size = min(256, span - first)
            pieces = []
            for c in range(comps):
                top = (s * comps + c) * LANES
                for q in range(whole):
                    left = first + (whole - q) * LANES
                    pieces.append(hankel[top : top + LANES, left : left + size])
                pieces.append(hankel[top : top + tail, first : first + size])
            product = jnp.dot(bank, jnp.concatenate(pieces, axis=0), preferred_element_type=jnp.float32)
            product = product * scale * inverse[:, first : first + size]
            for x in range(size // LANES):
                for g in range(0, count, 8):
                    aligned[pl.ds((s * count + g) * pitch + first // LANES + x, 8, stride=pitch), :] = product[
                        g : g + 8, x * LANES : (x + 1) * LANES
                    ]

    lane = lax.broadcasted_iota(jnp.int32, (block_rows, LANES), 1)
    for t in range(count):
        for b in range(rows // block_rows):
            total = None
            for s in range(stations):
                move = moves[s, t]
                high = lax.shift_right_logical(move, 7)
                low = lax.bitwise_and(move, LANES - 1)
                at = (s * count + t) * pitch + b * block_rows + high
                here = aligned[pl.ds(at, block_rows), :]
                after = aligned[pl.ds(at + 1, block_rows), :]
                merged = jnp.where(lane >= low, here, after)
                turned = pltpu.roll(merged, lax.rem(LANES - low, LANES), 1)
                term = flags[s, b].astype(jnp.float32) * turned
                total = term if total is None else total + term
            sums[t * rows + b * block_rows : t * rows + (b + 1) * block_rows, :] = total

    for x in range(rows):
        for g in range(0, count, 8):
            out_ref[g : g + 8, x * LANES : (x + 1) * LANES] = sums[pl.ds(g * rows + x, 8, stride=rows), :]


def shards(data, templates, moveouts, mask):
    stations, comps, samples = data.shape
    count, length = templates.shape[1], templates.shape[3]
    trailing = length + MOVE - 1
    blocks = mask.shape[1]
    block_len = samples // blocks
    following = shifted(data[:, :, :trailing], "tm", -1)
    width = -(-(samples + trailing) // LANES) * LANES + LANES
    wave = jnp.concatenate(
        [data, following, jnp.zeros((stations, comps, width - samples - trailing), data.dtype)], axis=2
    )
    bank = templates[..., ::-1].reshape(stations, count, comps * length)
    rows = samples // LANES
    pitch = -(-(rows + MOVE // LANES + 2) // 8) * 8
    sizes = (stations, comps, length, count, samples, block_len)
    partial = pl.pallas_call(
        functools.partial(correlate, sizes=sizes),
        out_shape=jax.ShapeDtypeStruct((count, samples), jnp.float32),
        in_specs=[
            pl.BlockSpec(memory_space=pltpu.SMEM),
            pl.BlockSpec(memory_space=pltpu.SMEM),
            pl.BlockSpec(memory_space=pltpu.VMEM),
            pl.BlockSpec(memory_space=pltpu.VMEM),
        ],
        out_specs=pl.BlockSpec(memory_space=pltpu.VMEM),
        scratch_shapes=[
            pltpu.VMEM((stations * comps * LANES, width), jnp.bfloat16),
            pltpu.VMEM((stations * count * pitch, LANES), jnp.float32),
            pltpu.VMEM((count * rows, LANES), jnp.float32),
        ],
        compiler_params=pltpu.CompilerParams(vmem_limit_bytes=40 * 2**20),
        name="correlate",
    )(moveouts, mask, wave, bank)

    live = jnp.sum(mask.astype(jnp.float32), axis=0)
    number = lax.axis_size("sta")
    if number > 4:
        summed, counts = lax.psum((partial, live), "sta")
    else:
        coded = (partial * WIRE_SCALE).astype(jnp.float16)
        summed, counts = partial, live
        for step in range(1, number):
            pairs = [(k, k ^ step) for k in range(number)]
            counts = counts + lax.ppermute(live, "sta", pairs)
        for step in range(number - 1, 0, -1):
            pairs = [(k, k ^ step) for k in range(number)]
            summed = summed + lax.ppermute(coded, "sta", pairs).astype(jnp.float32) * (1.0 / WIRE_SCALE)
    factor = math.sqrt(comps * length) * lax.rsqrt(counts)
    return summed * jnp.repeat(factor, block_len)[None, :]


def solution(mesh):
    placed = (
        P(("grp", "sta"), None, "tm"),
        P(("grp", "sta"), "comp", None, None),
        P(("grp", "sta"), "comp"),
        P(("grp", "sta"), "tm"),
    )
    return jax.shard_map(
        shards, mesh=mesh, in_specs=placed, out_specs=P(("grp", "comp"), "tm"), check_vma=False
    )
```

```python
import functools
import math

import jax
import jax.numpy as jnp
from jax import lax
from jax.experimental import pallas as pl
from jax.experimental.pallas import tpu as pltpu
from jax.sharding import PartitionSpec as P

MOVE = 625

eps_energy = 1e-06
LANES = 128
GROUP = 16
WIRE_SCALE = 2.0**13


def from_next(value, axis):
    count = lax.axis_size(axis)
    arrived = lax.ppermute(value, axis, [(k, (k - 1) % count) for k in range(count)])
    return jnp.where(lax.axis_index(axis) == count - 1, jnp.zeros_like(arrived), arrived)


def turn_groups(rows):
    width = rows.shape[1]
    source = lax.broadcasted_iota(jnp.int32, (width, width), 0)
    target = lax.broadcasted_iota(jnp.int32, (width, width), 1)
    swap = jnp.where(source == (target // GROUP) * GROUP + (GROUP - 1 - target % GROUP), 1.0, 0.0)
    return jnp.dot(rows, swap.astype(rows.dtype), preferred_element_type=jnp.float32).astype(rows.dtype)


def prepare(bank_ref, turned_ref, scale_ref):
    stations, comps, count, taps = bank_ref.shape
    whole = taps // LANES
    tail = taps - whole * LANES
    chunks = []
    for s in range(stations):
        energy = None
        for c in range(comps):
            wide = bank_ref[s, c].astype(jnp.float32)
            term = jnp.sum(wide * wide, axis=1, keepdims=True)
            energy = term if energy is None else energy + term
            for q in range(whole):
                chunks.append(bank_ref[s, c, :, q * LANES : (q + 1) * LANES])
        scale_ref[s] = jnp.broadcast_to(lax.rsqrt(energy + eps_energy), (count, LANES))
    turned = turn_groups(jnp.concatenate(chunks, axis=0))
    for s in range(stations):
        for n in range(comps * whole):
            first = (s * comps * whole + n) * count
            turned_ref[s, :, n * LANES : (n + 1) * LANES] = turned[first : first + count]
        for c in range(comps):
            left = comps * whole * LANES + c * tail
            turned_ref[s, :, left : left + tail] = turn_groups(bank_ref[s, c, :, whole * LANES :])


def fill_hankel(window, hankel, stations, comps):
    for s in range(stations):
        for c in range(comps):
            line = window(s, c)
            width = line.shape[1]
            base = jnp.broadcast_to(line, (GROUP, width))
            for g in range(LANES // GROUP):
                amount = (width - GROUP * g - (GROUP - 1)) % width
                top = (s * comps + c) * LANES + GROUP * g
                hankel[top : top + GROUP, :] = pltpu.roll(base, amount, 1, stride=1, stride_axis=0)


def window_energy(square, taps):
    width = square.shape[1]
    sums, size = {1: square}, 1
    while 2 * size <= taps:
        sums[2 * size] = sums[size] + pltpu.roll(sums[size], width - size, 1)
        size *= 2
    energy, start = None, 0
    for size in sorted(sums, reverse=True):
        if start + size <= taps:
            piece = sums[size] if start == 0 else pltpu.roll(sums[size], width - start, 1)
            energy = piece if energy is None else energy + piece
            start += size
    return energy


def inverse_energy(square, taps):
    energy = window_energy(square, taps)
    return jnp.where(energy > 0.0, lax.rsqrt(energy + eps_energy), 0.0)


def products(inverse, turned_ref, scale_ref, hankel, taps, comps, tiles, put):
    stations, count, depth = turned_ref.shape
    whole = taps // LANES
    tail = taps - whole * LANES
    span = tiles * LANES
    for s in range(stations):
        pieces = []
        for c in range(comps):
            top = (s * comps + c) * LANES
            for q in range(whole):
                pieces.append(hankel[top : top + LANES, q * LANES : q * LANES + span])
        for c in range(comps):
            top = (s * comps + c) * LANES
            pieces.append(hankel[top : top + tail, whole * LANES : whole * LANES + span])
        product = jnp.dot(turned_ref[s], jnp.concatenate(pieces, axis=0), preferred_element_type=jnp.float32)
        product = product * inverse[s : s + 1, :span]
        for x in range(tiles):
            for g in range(0, count, 8):
                tile = product[g : g + 8, x * LANES : (x + 1) * LANES] * scale_ref[s, g : g + 8, :]
                put(s * count + g, x, tile)


def align(moves, flags, block, aligned, sums, out_ref, rows):
    stations, count = moves.shape
    pitch = aligned.shape[0] // (stations * count)
    lane = lax.broadcasted_iota(jnp.int32, (rows, LANES), 1)
    for t in range(count):
        total = None
        for s in range(stations):
            move = moves[s, t]
            high = lax.shift_right_logical(move, 7)
            low = lax.bitwise_and(move, LANES - 1)
            at = (s * count + t) * pitch + high
            merged = jnp.where(lane >= low, aligned[pl.ds(at, rows), :], aligned[pl.ds(at + 1, rows), :])
            term = flags[s, block].astype(jnp.float32) * pltpu.roll(merged, LANES - low, 1)
            total = term if total is None else total + term
        sums[t * rows : (t + 1) * rows, :] = total
    for x in range(rows):
        for g in range(0, count, 8):
            out_ref[g : g + 8, x * LANES : (x + 1) * LANES] = sums[pl.ds(g * rows + x, 8, stride=rows), :]


def put_counts(flags, out_ref, left):
    lane = lax.broadcasted_iota(jnp.int32, (out_ref.shape[0], LANES), 1)
    counts = jnp.zeros(lane.shape, jnp.float32)
    for b in range(flags.shape[1]):
        live = sum(flags[s, b] for s in range(flags.shape[0])).astype(jnp.float32)
        counts = jnp.where(lane == b, live, counts)
    out_ref[:, left : left + LANES] = counts


def first_block(
    moves, flags, wave_hbm, bank_hbm, out_ref, later_ref, turned_ref, scale_ref, kept_ref,
    wave_ref, bank_ref, hankel, aligned, sums, ready,
):
    comps, stations, samples = wave_ref.shape
    count, taps = bank_ref.shape[2:]
    rows = sums.shape[0] // count
    length = rows * LANES
    pitch = aligned.shape[0] // (stations * count)
    kept = kept_ref.shape[0] // (stations * count)
    wave_copy = pltpu.make_async_copy(wave_hbm, wave_ref, ready.at[0])
    bank_copy = pltpu.make_async_copy(bank_hbm, bank_ref, ready.at[1])
    wave_copy.start()
    bank_copy.start()
    put_counts(flags, out_ref, length)
    wave_copy.wait()
    bank_copy.wait()
    later_ref[...] = wave_ref[:, :, samples - later_ref.shape[2] :]

    def window(s, c):
        return wave_ref[c, s : s + 1, : 2 * length]

    fill_hankel(window, hankel, stations, comps)
    wide = wave_ref[:, :, : 2 * length].astype(jnp.float32)
    inverse = inverse_energy(jnp.sum(wide * wide, axis=0), taps)
    prepare(bank_ref, turned_ref, scale_ref)

    def put(first, x, tile):
        aligned[pl.ds(first * pitch + x, 8, stride=pitch), :] = tile
        if rows <= x < rows + kept:
            kept_ref[pl.ds(first * kept + x - rows, 8, stride=kept), :] = tile

    products(inverse, turned_ref, scale_ref, hankel, taps, comps, pitch, put)
    align(moves, flags, 0, aligned, sums, out_ref, rows)


def last_block(
    moves, flags, later_ref, next_ref, turned_ref, scale_ref, kept_ref, out_ref, hankel, aligned, sums, *, taps
):
    comps, stations, own = later_ref.shape
    count, length = out_ref.shape
    rows = length // LANES
    pitch = aligned.shape[0] // (stations * count)
    kept = kept_ref.shape[0] // (stations * count)

    def window(s, c):
        return jnp.concatenate([later_ref[c, s : s + 1, :], next_ref[c, s : s + 1, :length]], axis=1)

    fill_hankel(window, hankel, stations, comps)
    squares = [jnp.sum(part * part, axis=0) for part in (later_ref[...].astype(jnp.float32), next_ref[:, :, :length].astype(jnp.float32))]
    inverse = inverse_energy(jnp.concatenate(squares, axis=1), taps)
    for first in range(0, stations * count, 8):
        for x in range(kept):
            aligned[pl.ds(first * pitch + x, 8, stride=pitch), :] = kept_ref[pl.ds(first * kept + x, 8, stride=kept), :]

    def put(first, x, tile):
        aligned[pl.ds(first * pitch + kept + x, 8, stride=pitch), :] = tile

    products(inverse, turned_ref, scale_ref, hankel, taps, comps, pitch - kept, put)
    align(moves, flags, flags.shape[1] - 1, aligned, sums, out_ref, rows)


def finish(first_ref, last_ref, near_ref, far_ref, out_ref, *, factor):
    length = last_ref.shape[1]
    counts = first_ref[:, length:] + near_ref[:, length : length + LANES]
    lane = lax.broadcasted_iota(jnp.int32, counts.shape, 1)
    sums = first_ref[:, :length] + near_ref[:, :length], last_ref[...] + near_ref[:, length + LANES :] + far_ref[...]
    for b, total in enumerate(sums):
        count = jnp.sum(jnp.where(lane == b, counts, 0.0), axis=1, keepdims=True)
        out_ref[:, b * length : (b + 1) * length] = total * (factor * lax.rsqrt(count))


def shards(data, templates, moveouts, mask):
    stations, comps, samples = data.shape
    count, taps = templates.shape[1], templates.shape[3]
    blocks = mask.shape[1]
    length = samples // blocks
    assert blocks == 2 and length >= taps + MOVE - 1
    wave_own = jnp.transpose(data, (1, 0, 2))
    wave = pltpu.with_memory_space_constraint(wave_own, pltpu.HBM)
    bank = pltpu.with_memory_space_constraint(jnp.transpose(templates, (0, 2, 1, 3)), pltpu.HBM)
    following = from_next(wave_own, "tm")

    rows = length // LANES
    pitch = rows + -(-(MOVE - 1) // LANES)
    kept = (2 * length - taps + 1) // LANES - rows
    smem, vmem = pl.BlockSpec(memory_space=pltpu.SMEM), pl.BlockSpec(memory_space=pltpu.VMEM)
    hbm = pl.BlockSpec(memory_space=pltpu.HBM)
    last_width = 2 * length - kept * LANES

    def scratch(width):
        return [
            pltpu.VMEM((stations * comps * LANES, width), jnp.bfloat16),
            pltpu.VMEM((stations * count * pitch, LANES), jnp.float32),
            pltpu.VMEM((count * rows, LANES), jnp.float32),
        ]

    params = pltpu.CompilerParams(vmem_limit_bytes=32 * 2**20)
    first, later, turned, scale, both = pl.pallas_call(
        first_block,
        out_shape=(
            jax.ShapeDtypeStruct((count, length + LANES), jnp.float32),
            jax.ShapeDtypeStruct((comps, stations, last_width - length), jnp.bfloat16),
            jax.ShapeDtypeStruct((stations, count, comps * taps), jnp.bfloat16),
            jax.ShapeDtypeStruct((stations, count, LANES), jnp.float32),
            jax.ShapeDtypeStruct((stations * count * kept, LANES), jnp.float32),
        ),
        in_specs=[smem, smem, hbm, hbm],
        out_specs=(vmem, vmem, vmem, vmem, vmem),
        scratch_shapes=[pltpu.VMEM(wave.shape, wave.dtype), pltpu.VMEM(bank.shape, bank.dtype)]
        + scratch(2 * length)
        + [pltpu.SemaphoreType.DMA((2,))],
        compiler_params=params,
        name="first_block",
    )(moveouts, mask, wave, bank)
    last = pl.pallas_call(
        functools.partial(last_block, taps=taps),
        out_shape=jax.ShapeDtypeStruct((count, length), jnp.float32),
        in_specs=[smem, smem, vmem, vmem, vmem, vmem, vmem],
        out_specs=vmem,
        scratch_shapes=scratch(last_width),
        compiler_params=params,
        name="last_block",
    )(moveouts, mask, later, following, turned, scale, both)

    number = lax.axis_size("sta")
    if number != 4:
        first, last = lax.psum((first, last), "sta")
        counts = first[:1, length:]
        gain = [math.sqrt(comps * taps) * lax.rsqrt(counts[:, b : b + 1]) for b in range(blocks)]
        return jnp.concatenate([first[:, :length] * gain[0], last * gain[1]], axis=1)

    def exchange(part, step):
        return lax.ppermute(part, "sta", [(k, k ^ step) for k in range(number)])

    def code(part):
        return (part * WIRE_SCALE).astype(jnp.float16)

    def decode(part):
        return part.astype(jnp.float32) * (1.0 / WIRE_SCALE)

    coded_last = code(last)
    far_first = exchange(code(first), 2)
    far = [exchange(coded_last, step) for step in (3, 2)]
    first = first + decode(far_first)
    near = exchange(jnp.concatenate([code(first), coded_last], axis=1), 1)
    return pl.pallas_call(
        functools.partial(finish, factor=math.sqrt(comps * taps)),
        out_shape=jax.ShapeDtypeStruct((count, samples), jnp.float32),
        in_specs=[vmem] * 4,
        out_specs=vmem,
        compiler_params=params,
        name="finish",
    )(first, last, decode(near), decode(far[0]) + decode(far[1]))


def solution(mesh):
    placed = (
        P(("grp", "sta"), None, "tm"),
        P(("grp", "sta"), "comp", None, None),
        P(("grp", "sta"), "comp"),
        P(("grp", "sta"), "tm"),
    )
    return jax.shard_map(
        shards, mesh=mesh, in_specs=placed, out_specs=P(("grp", "comp"), "tm"), check_vma=False
    )
```

```python
import functools
import math

import jax
import jax.numpy as jnp
from jax import lax
from jax.experimental import pallas as pl
from jax.experimental.pallas import tpu as pltpu
from jax.sharding import PartitionSpec as P

MOVE = 625

eps_energy = 1e-06
LANES = 128
GROUP = 16
COUNT_ROWS = 8
WIRE_SCALE = 2.0**13


def from_next(value, axis):
    count = lax.axis_size(axis)
    arrived = lax.ppermute(value, axis, [(k, (k - 1) % count) for k in range(count)])
    return jnp.where(lax.axis_index(axis) == count - 1, jnp.zeros_like(arrived), arrived)


def turn_groups(rows):
    width = rows.shape[1]
    source = lax.broadcasted_iota(jnp.int32, (width, width), 0)
    target = lax.broadcasted_iota(jnp.int32, (width, width), 1)
    swap = jnp.where(source == (target // GROUP) * GROUP + (GROUP - 1 - target % GROUP), 1.0, 0.0)
    return jnp.dot(rows, swap.astype(rows.dtype), preferred_element_type=jnp.float32).astype(rows.dtype)


def prepare(bank_ref, turned_ref, scale_ref):
    stations, comps, count, taps = bank_ref.shape
    whole = taps // LANES
    tail = taps - whole * LANES
    chunks = []
    for s in range(stations):
        energy = None
        for c in range(comps):
            wide = bank_ref[s, c].astype(jnp.float32)
            term = jnp.sum(wide * wide, axis=1, keepdims=True)
            energy = term if energy is None else energy + term
            for q in range(whole):
                chunks.append(bank_ref[s, c, :, q * LANES : (q + 1) * LANES])
        scale_ref[s] = jnp.broadcast_to(lax.rsqrt(energy + eps_energy), (count, LANES))
    turned = turn_groups(jnp.concatenate(chunks, axis=0))
    for s in range(stations):
        for n in range(comps * whole):
            first = (s * comps * whole + n) * count
            turned_ref[s, :, n * LANES : (n + 1) * LANES] = turned[first : first + count]
        for c in range(comps):
            left = comps * whole * LANES + c * tail
            turned_ref[s, :, left : left + tail] = turn_groups(bank_ref[s, c, :, whole * LANES :])


def fill_hankel(window, hankel, stations, comps):
    for s in range(stations):
        for c in range(comps):
            line = window(s, c)
            width = line.shape[1]
            base = jnp.broadcast_to(line, (GROUP, width))
            for g in range(LANES // GROUP):
                amount = (width - GROUP * g - (GROUP - 1)) % width
                top = (s * comps + c) * LANES + GROUP * g
                hankel[top : top + GROUP, :] = pltpu.roll(base, amount, 1, stride=1, stride_axis=0)


def window_energy(square, taps):
    width = square.shape[1]
    sums, size = {1: square}, 1
    while 2 * size <= taps:
        sums[2 * size] = sums[size] + pltpu.roll(sums[size], width - size, 1)
        size *= 2
    energy, start = None, 0
    for size in sorted(sums, reverse=True):
        if start + size <= taps:
            piece = sums[size] if start == 0 else pltpu.roll(sums[size], width - start, 1)
            energy = piece if energy is None else energy + piece
            start += size
    return energy


def inverse_energy(square, taps):
    energy = window_energy(square, taps)
    return jnp.where(energy > 0.0, lax.rsqrt(energy + eps_energy), 0.0)


def products(inverse, turned_ref, scale_ref, hankel, taps, comps, tiles, put):
    stations, count, depth = turned_ref.shape
    whole = taps // LANES
    tail = taps - whole * LANES
    span = tiles * LANES
    for s in range(stations):
        pieces = []
        for c in range(comps):
            top = (s * comps + c) * LANES
            for q in range(whole):
                pieces.append(hankel[top : top + LANES, q * LANES : q * LANES + span])
        for c in range(comps):
            top = (s * comps + c) * LANES
            pieces.append(hankel[top : top + tail, whole * LANES : whole * LANES + span])
        product = jnp.dot(turned_ref[s], jnp.concatenate(pieces, axis=0), preferred_element_type=jnp.float32)
        product = product * inverse[s : s + 1, :span]
        for x in range(tiles):
            for g in range(0, count, 8):
                tile = product[g : g + 8, x * LANES : (x + 1) * LANES] * scale_ref[s, g : g + 8, :]
                put(s * count + g, x, tile)


def align(moves, flags, block, aligned, out_ref, rows):
    stations, count = moves.shape
    pitch = aligned.shape[0] // (stations * count)
    lane = lax.broadcasted_iota(jnp.int32, (rows, LANES), 1)
    for t in range(count):
        total = None
        for s in range(stations):
            move = moves[s, t]
            high = lax.shift_right_logical(move, 7)
            low = lax.bitwise_and(move, LANES - 1)
            at = (s * count + t) * pitch + high
            merged = jnp.where(lane >= low, aligned[pl.ds(at, rows), :], aligned[pl.ds(at + 1, rows), :])
            term = flags[s, block].astype(jnp.float32) * pltpu.roll(merged, LANES - low, 1)
            total = term if total is None else total + term
        out_ref[t * rows : (t + 1) * rows, :] = total


def put_counts(flags, out_ref, top):
    lane = lax.broadcasted_iota(jnp.int32, (COUNT_ROWS, LANES), 1)
    counts = jnp.zeros(lane.shape, jnp.float32)
    for b in range(flags.shape[1]):
        live = sum(flags[s, b] for s in range(flags.shape[0])).astype(jnp.float32)
        counts = jnp.where(lane == b, live, counts)
    out_ref[top : top + COUNT_ROWS, :] = counts


def fetch(pairs, ready):
    copies = [pltpu.make_async_copy(source, target, ready.at[n]) for n, (source, target) in enumerate(pairs)]
    for copy in copies:
        copy.start()
    return copies


def first_block(
    moves_hbm, flags_hbm, wave_hbm, bank_hbm, out_ref, later_ref, turned_ref, scale_ref, kept_ref,
    wave_ref, bank_ref, moves, flags, hankel, aligned, ready,
):
    comps, stations, samples = wave_ref.shape
    count, taps = bank_ref.shape[2:]
    rows = (out_ref.shape[0] - COUNT_ROWS) // count
    length = rows * LANES
    pitch = aligned.shape[0] // (stations * count)
    kept = kept_ref.shape[0] // (stations * count)
    copies = fetch(((wave_hbm, wave_ref), (bank_hbm, bank_ref), (moves_hbm, moves), (flags_hbm, flags)), ready)
    for copy in copies:
        copy.wait()
    put_counts(flags, out_ref, count * rows)
    later_ref[...] = wave_ref[:, :, samples - later_ref.shape[2] :]

    def window(s, c):
        return wave_ref[c, s : s + 1, : 2 * length]

    fill_hankel(window, hankel, stations, comps)
    wide = wave_ref[:, :, : 2 * length].astype(jnp.float32)
    inverse = inverse_energy(jnp.sum(wide * wide, axis=0), taps)
    prepare(bank_ref, turned_ref, scale_ref)

    def put(first, x, tile):
        aligned[pl.ds(first * pitch + x, 8, stride=pitch), :] = tile
        if rows <= x < rows + kept:
            kept_ref[pl.ds(first * kept + x - rows, 8, stride=kept), :] = tile

    products(inverse, turned_ref, scale_ref, hankel, taps, comps, pitch, put)
    align(moves, flags, 0, aligned, out_ref, rows)


def last_block(
    moves_hbm, flags_hbm, later_ref, next_ref, turned_ref, scale_ref, kept_ref, out_ref,
    moves, flags, hankel, aligned, ready, *, taps,
):
    comps, stations, own = later_ref.shape
    count = scale_ref.shape[1]
    rows = out_ref.shape[0] // count
    length = rows * LANES
    pitch = aligned.shape[0] // (stations * count)
    kept = kept_ref.shape[0] // (stations * count)
    copies = fetch(((moves_hbm, moves), (flags_hbm, flags)), ready)

    def window(s, c):
        return jnp.concatenate([later_ref[c, s : s + 1, :], next_ref[c, s : s + 1, :length]], axis=1)

    fill_hankel(window, hankel, stations, comps)
    squares = [jnp.sum(part * part, axis=0) for part in (later_ref[...].astype(jnp.float32), next_ref[:, :, :length].astype(jnp.float32))]
    inverse = inverse_energy(jnp.concatenate(squares, axis=1), taps)
    for first in range(0, stations * count, 8):
        for x in range(kept):
            aligned[pl.ds(first * pitch + x, 8, stride=pitch), :] = kept_ref[pl.ds(first * kept + x, 8, stride=kept), :]

    def put(first, x, tile):
        aligned[pl.ds(first * pitch + kept + x, 8, stride=pitch), :] = tile

    products(inverse, turned_ref, scale_ref, hankel, taps, comps, pitch - kept, put)
    for copy in copies:
        copy.wait()
    align(moves, flags, flags.shape[1] - 1, aligned, out_ref, rows)


def finish(first_ref, near_ref, last_ref, far_ref, out_ref, sums, *, factor):
    count, samples = out_ref.shape
    size = last_ref.shape[0]
    rows = size // count
    counts = first_ref[size:, :] + near_ref[size:, :]
    lane = lax.broadcasted_iota(jnp.int32, counts.shape, 1)
    for b, (own_ref, other_ref) in enumerate(((first_ref, near_ref), (last_ref, far_ref))):
        live = jnp.sum(jnp.where(lane == b, counts, 0.0), axis=1, keepdims=True)
        gain = jnp.broadcast_to(factor * lax.rsqrt(live), (COUNT_ROWS, LANES))
        for top in range(0, size, COUNT_ROWS):
            part = slice(top, top + COUNT_ROWS)
            sums[part, :] = (own_ref[part, :] + other_ref[part, :]) * gain
        for x in range(rows):
            left = (b * rows + x) * LANES
            for g in range(0, count, 8):
                out_ref[g : g + 8, left : left + LANES] = sums[pl.ds(g * rows + x, 8, stride=rows), :]


def shards(data, templates, moveouts, mask):
    stations, comps, samples = data.shape
    count, taps = templates.shape[1], templates.shape[3]
    blocks = mask.shape[1]
    length = samples // blocks
    assert blocks == 2 and length >= taps + MOVE - 1
    wave_own = jnp.transpose(data, (1, 0, 2))
    wave = pltpu.with_memory_space_constraint(wave_own, pltpu.HBM)
    bank = pltpu.with_memory_space_constraint(jnp.transpose(templates, (0, 2, 1, 3)), pltpu.HBM)
    following = from_next(wave_own, "tm")

    rows = length // LANES
    pitch = rows + -(-(MOVE - 1) // LANES)
    kept = (2 * length - taps + 1) // LANES - rows
    vmem = pl.BlockSpec(memory_space=pltpu.VMEM)
    hbm = pl.BlockSpec(memory_space=pl.ANY)
    last_width = 2 * length - kept * LANES

    def scratch(width):
        return [
            pltpu.SMEM(moveouts.shape, moveouts.dtype),
            pltpu.SMEM(mask.shape, mask.dtype),
            pltpu.VMEM((stations * comps * LANES, width), jnp.bfloat16),
            pltpu.VMEM((stations * count * pitch, LANES), jnp.float32),
        ]

    params = pltpu.CompilerParams(vmem_limit_bytes=32 * 2**20)
    first, later, turned, scale, both = pl.pallas_call(
        first_block,
        out_shape=(
            jax.ShapeDtypeStruct((count * rows + COUNT_ROWS, LANES), jnp.float32),
            jax.ShapeDtypeStruct((comps, stations, last_width - length), jnp.bfloat16),
            jax.ShapeDtypeStruct((stations, count, comps * taps), jnp.bfloat16),
            jax.ShapeDtypeStruct((stations, count, LANES), jnp.float32),
            jax.ShapeDtypeStruct((stations * count * kept, LANES), jnp.float32),
        ),
        in_specs=[hbm] * 4,
        out_specs=(vmem, vmem, vmem, vmem, vmem),
        scratch_shapes=[pltpu.VMEM(wave.shape, wave.dtype), pltpu.VMEM(bank.shape, bank.dtype)]
        + scratch(2 * length)
        + [pltpu.SemaphoreType.DMA((4,))],
        compiler_params=params,
        name="first_block",
    )(moveouts, mask, wave, bank)
    last = pl.pallas_call(
        functools.partial(last_block, taps=taps),
        out_shape=jax.ShapeDtypeStruct((count * rows, LANES), jnp.float32),
        in_specs=[hbm] * 2 + [vmem] * 5,
        out_specs=vmem,
        scratch_shapes=scratch(last_width) + [pltpu.SemaphoreType.DMA((2,))],
        compiler_params=params,
        name="last_block",
    )(moveouts, mask, later, following, turned, scale, both)

    number = lax.axis_size("sta")

    def exchange(part, step):
        return lax.ppermute(part, "sta", [(k, k ^ step) for k in range(number)])

    def code(part):
        return (part * WIRE_SCALE).astype(jnp.float16)

    def decode(part):
        return part.astype(jnp.float32) * (1.0 / WIRE_SCALE)

    if number == 4:
        far_first = exchange(code(first), 2)
        coded_last = code(last)
        far = [exchange(coded_last, step) for step in (3, 2, 1)]
        first = first + decode(far_first)
        near = decode(exchange(code(first), 1))
        far = decode(far[0]) + decode(far[1]) + decode(far[2])
    else:
        first, last = lax.psum((first, last), "sta")
        near, far = jnp.zeros_like(first), jnp.zeros_like(last)
    return pl.pallas_call(
        functools.partial(finish, factor=math.sqrt(comps * taps)),
        out_shape=jax.ShapeDtypeStruct((count, samples), jnp.float32),
        in_specs=[vmem] * 4,
        out_specs=vmem,
        scratch_shapes=[pltpu.VMEM((count * rows, LANES), jnp.float32)],
        compiler_params=params,
        name="finish",
    )(first, near, last, far)


def solution(mesh):
    placed = (
        P(("grp", "sta"), None, "tm"),
        P(("grp", "sta"), "comp", None, None),
        P(("grp", "sta"), "comp"),
        P(("grp", "sta"), "tm"),
    )
    return jax.shard_map(
        shards, mesh=mesh, in_specs=placed, out_specs=P(("grp", "comp"), "tm"), check_vma=False
    )
```

```python
import functools
import math

import jax
import jax.numpy as jnp
from jax import lax
from jax.experimental import pallas as pl
from jax.experimental.pallas import tpu as pltpu
from jax.sharding import PartitionSpec as P

MOVE = 625

eps_energy = 1e-06
LANES = 128
GROUP = 16
COUNT_ROWS = 8
TILES = 4
WIRE_SCALE = 2.0**13


def from_next(value, axis):
    count = lax.axis_size(axis)
    arrived = lax.ppermute(value, axis, [(k, (k - 1) % count) for k in range(count)])
    return jnp.where(lax.axis_index(axis) == count - 1, jnp.zeros_like(arrived), arrived)


def turn_groups(rows):
    width = rows.shape[1]
    source = lax.broadcasted_iota(jnp.int32, (width, width), 0)
    target = lax.broadcasted_iota(jnp.int32, (width, width), 1)
    swap = jnp.where(source == (target // GROUP) * GROUP + (GROUP - 1 - target % GROUP), 1.0, 0.0)
    return jnp.dot(rows, swap.astype(rows.dtype), preferred_element_type=jnp.float32).astype(rows.dtype)


def prepare(bank_ref, turned_ref, scale_ref):
    stations, comps, count, taps = bank_ref.shape
    whole = taps // LANES
    tail = taps - whole * LANES
    chunks = []
    for s in range(stations):
        energy = None
        for c in range(comps):
            wide = bank_ref[s, c].astype(jnp.float32)
            term = jnp.sum(wide * wide, axis=1, keepdims=True)
            energy = term if energy is None else energy + term
            for q in range(whole):
                chunks.append(bank_ref[s, c, :, q * LANES : (q + 1) * LANES])
        scale_ref[s] = jnp.broadcast_to(lax.rsqrt(energy + eps_energy), (count, LANES))
    turned = turn_groups(jnp.concatenate(chunks, axis=0))
    for s in range(stations):
        for n in range(comps * whole):
            first = (s * comps * whole + n) * count
            turned_ref[s, :, n * LANES : (n + 1) * LANES] = turned[first : first + count]
        for c in range(comps):
            left = comps * whole * LANES + c * tail
            turned_ref[s, :, left : left + tail] = turn_groups(bank_ref[s, c, :, whole * LANES :])


def fill_hankel(window, hankel, stations, comps):
    for s in range(stations):
        for c in range(comps):
            line = window(s, c)
            width = line.shape[1]
            base = jnp.broadcast_to(line, (GROUP, width))
            for g in range(LANES // GROUP):
                amount = (width - GROUP * g - (GROUP - 1)) % width
                top = (s * comps + c) * LANES + GROUP * g
                hankel[top : top + GROUP, :] = pltpu.roll(base, amount, 1, stride=1, stride_axis=0)


def window_energy(square, taps):
    width = square.shape[1]
    sums, size = {1: square}, 1
    while 2 * size <= taps:
        sums[2 * size] = sums[size] + pltpu.roll(sums[size], width - size, 1)
        size *= 2
    energy, start = None, 0
    for size in sorted(sums, reverse=True):
        if start + size <= taps:
            piece = sums[size] if start == 0 else pltpu.roll(sums[size], width - start, 1)
            energy = piece if energy is None else energy + piece
            start += size
    return energy


def inverse_energy(square, taps):
    energy = window_energy(square, taps)
    return jnp.where(energy > 0.0, lax.rsqrt(energy + eps_energy), 0.0)


def products(inverse, turned_ref, scale_ref, hankel, taps, comps, tiles, put):
    stations, count, depth = turned_ref.shape
    whole = taps // LANES
    tail = taps - whole * LANES
    for s in range(stations):
        tops = [(s * comps + c) * LANES for c in range(comps)]
        for first in range(0, tiles, TILES):
            size = min(TILES, tiles - first)

            def part(top, rows, q):
                return hankel[top : top + rows, (first + q) * LANES : (first + q + size) * LANES]

            pieces = [part(top, LANES, q) for top in tops for q in range(whole)]
            pieces += [part(top, tail, whole) for top in tops]
            product = jnp.dot(turned_ref[s], jnp.concatenate(pieces, axis=0), preferred_element_type=jnp.float32)
            product = product * inverse[s : s + 1, first * LANES : (first + size) * LANES]
            for x in range(size):
                for g in range(0, count, 8):
                    tile = product[g : g + 8, x * LANES : (x + 1) * LANES] * scale_ref[s, g : g + 8, :]
                    put(s * count + g, first + x, tile)


def align(moves, flags, block, aligned, out_ref, rows):
    stations, count = moves.shape
    pitch = aligned.shape[0] // (stations * count)
    lane = lax.broadcasted_iota(jnp.int32, (rows, LANES), 1)
    for t in range(count):
        total = None
        for s in range(stations):
            move = moves[s, t]
            high = lax.shift_right_logical(move, 7)
            low = lax.bitwise_and(move, LANES - 1)
            at = (s * count + t) * pitch + high
            merged = jnp.where(lane >= low, aligned[pl.ds(at, rows), :], aligned[pl.ds(at + 1, rows), :])
            term = flags[s, block].astype(jnp.float32) * pltpu.roll(merged, LANES - low, 1)
            total = term if total is None else total + term
        out_ref[t * rows : (t + 1) * rows, :] = total


def put_counts(flags, out_ref, top):
    lane = lax.broadcasted_iota(jnp.int32, (COUNT_ROWS, LANES), 1)
    counts = jnp.zeros(lane.shape, jnp.float32)
    for b in range(flags.shape[1]):
        live = sum(flags[s, b] for s in range(flags.shape[0])).astype(jnp.float32)
        counts = jnp.where(lane == b, live, counts)
    out_ref[top : top + COUNT_ROWS, :] = counts


def fetch(pairs, ready):
    copies = [pltpu.make_async_copy(source, target, ready.at[n]) for n, (source, target) in enumerate(pairs)]
    for copy in copies:
        copy.start()
    return copies


def first_block(
    moves_hbm, flags_hbm, wave_hbm, bank_hbm, out_ref, later_ref, turned_ref, scale_ref, kept_ref,
    wave_ref, bank_ref, moves, flags, hankel, aligned, ready,
):
    comps, stations, samples = wave_ref.shape
    count, taps = bank_ref.shape[2:]
    rows = (out_ref.shape[0] - COUNT_ROWS) // count
    length = rows * LANES
    pitch = aligned.shape[0] // (stations * count)
    kept = kept_ref.shape[0] // (stations * count)
    copies = fetch(((wave_hbm, wave_ref), (bank_hbm, bank_ref), (moves_hbm, moves), (flags_hbm, flags)), ready)
    for copy in copies:
        copy.wait()
    put_counts(flags, out_ref, count * rows)
    later_ref[...] = wave_ref[:, :, samples - later_ref.shape[2] :]

    def window(s, c):
        return wave_ref[c, s : s + 1, : 2 * length]

    fill_hankel(window, hankel, stations, comps)
    wide = wave_ref[:, :, : 2 * length].astype(jnp.float32)
    inverse = inverse_energy(jnp.sum(wide * wide, axis=0), taps)
    prepare(bank_ref, turned_ref, scale_ref)

    def put(first, x, tile):
        aligned[pl.ds(first * pitch + x, 8, stride=pitch), :] = tile
        if rows <= x < rows + kept:
            kept_ref[pl.ds(first * kept + x - rows, 8, stride=kept), :] = tile

    products(inverse, turned_ref, scale_ref, hankel, taps, comps, pitch, put)
    align(moves, flags, 0, aligned, out_ref, rows)


def last_block(
    moves_hbm, flags_hbm, later_ref, next_ref, turned_ref, scale_ref, kept_ref, out_ref,
    moves, flags, hankel, aligned, ready, *, taps,
):
    comps, stations, own = later_ref.shape
    count = scale_ref.shape[1]
    rows = out_ref.shape[0] // count
    length = rows * LANES
    pitch = aligned.shape[0] // (stations * count)
    kept = kept_ref.shape[0] // (stations * count)
    copies = fetch(((moves_hbm, moves), (flags_hbm, flags)), ready)

    def window(s, c):
        return jnp.concatenate([later_ref[c, s : s + 1, :], next_ref[c, s : s + 1, :length]], axis=1)

    fill_hankel(window, hankel, stations, comps)
    squares = [jnp.sum(part * part, axis=0) for part in (later_ref[...].astype(jnp.float32), next_ref[:, :, :length].astype(jnp.float32))]
    inverse = inverse_energy(jnp.concatenate(squares, axis=1), taps)
    for first in range(0, stations * count, 8):
        for x in range(kept):
            aligned[pl.ds(first * pitch + x, 8, stride=pitch), :] = kept_ref[pl.ds(first * kept + x, 8, stride=kept), :]

    def put(first, x, tile):
        aligned[pl.ds(first * pitch + kept + x, 8, stride=pitch), :] = tile

    products(inverse, turned_ref, scale_ref, hankel, taps, comps, pitch - kept, put)
    for copy in copies:
        copy.wait()
    align(moves, flags, flags.shape[1] - 1, aligned, out_ref, rows)


def finish(first_ref, near_ref, last_ref, far_ref, out_ref, sums, *, factor):
    count, samples = out_ref.shape
    size = last_ref.shape[0]
    rows = size // count
    counts = first_ref[size:, :] + near_ref[size:, :]
    lane = lax.broadcasted_iota(jnp.int32, counts.shape, 1)
    for b, (own_ref, other_ref) in enumerate(((first_ref, near_ref), (last_ref, far_ref))):
        live = jnp.sum(jnp.where(lane == b, counts, 0.0), axis=1, keepdims=True)
        gain = jnp.broadcast_to(factor * lax.rsqrt(live), (COUNT_ROWS, LANES))
        for top in range(0, size, COUNT_ROWS):
            part = slice(top, top + COUNT_ROWS)
            sums[part, :] = (own_ref[part, :] + other_ref[part, :]) * gain
        for x in range(rows):
            left = (b * rows + x) * LANES
            for g in range(0, count, 8):
                out_ref[g : g + 8, left : left + LANES] = sums[pl.ds(g * rows + x, 8, stride=rows), :]


def in_hbm(value):
    return pltpu.with_memory_space_constraint(value, pltpu.HBM)


def shards(data, templates, moveouts, mask):
    stations, comps, samples = data.shape
    count, taps = templates.shape[1], templates.shape[3]
    blocks = mask.shape[1]
    length = samples // blocks
    assert blocks == 2 and length >= taps + MOVE - 1
    wave_own = jnp.transpose(data, (1, 0, 2))
    wave = pltpu.with_memory_space_constraint(wave_own, pltpu.HBM)
    bank = pltpu.with_memory_space_constraint(jnp.transpose(templates, (0, 2, 1, 3)), pltpu.HBM)
    following = from_next(wave_own, "tm")

    rows = length // LANES
    pitch = rows + -(-(MOVE - 1) // LANES)
    kept = (2 * length - taps + 1) // LANES - rows
    vmem = pl.BlockSpec(memory_space=pltpu.VMEM)
    hbm = pl.BlockSpec(memory_space=pl.ANY)
    last_width = 2 * length - kept * LANES

    def scratch(width):
        return [
            pltpu.SMEM(moveouts.shape, moveouts.dtype),
            pltpu.SMEM(mask.shape, mask.dtype),
            pltpu.VMEM((stations * comps * LANES, width), jnp.bfloat16),
            pltpu.VMEM((stations * count * pitch, LANES), jnp.float32),
        ]

    params = pltpu.CompilerParams(vmem_limit_bytes=32 * 2**20)
    first, later, turned, scale, both = pl.pallas_call(
        first_block,
        out_shape=(
            jax.ShapeDtypeStruct((count * rows + COUNT_ROWS, LANES), jnp.float32),
            jax.ShapeDtypeStruct((comps, stations, last_width - length), jnp.bfloat16),
            jax.ShapeDtypeStruct((stations, count, comps * taps), jnp.bfloat16),
            jax.ShapeDtypeStruct((stations, count, LANES), jnp.float32),
            jax.ShapeDtypeStruct((stations * count * kept, LANES), jnp.float32),
        ),
        in_specs=[hbm] * 4,
        out_specs=(vmem, vmem, vmem, vmem, vmem),
        scratch_shapes=[pltpu.VMEM(wave.shape, wave.dtype), pltpu.VMEM(bank.shape, bank.dtype)]
        + scratch(2 * length)
        + [pltpu.SemaphoreType.DMA((4,))],
        compiler_params=params,
        name="first_block",
    )(in_hbm(moveouts), in_hbm(mask), wave, bank)
    last = pl.pallas_call(
        functools.partial(last_block, taps=taps),
        out_shape=jax.ShapeDtypeStruct((count * rows, LANES), jnp.float32),
        in_specs=[hbm] * 2 + [vmem] * 5,
        out_specs=vmem,
        scratch_shapes=scratch(last_width) + [pltpu.SemaphoreType.DMA((2,))],
        compiler_params=params,
        name="last_block",
    )(in_hbm(moveouts), in_hbm(mask), later, following, turned, scale, both)

    number = lax.axis_size("sta")

    def exchange(part, step):
        return lax.ppermute(part, "sta", [(k, k ^ step) for k in range(number)])

    def code(part):
        return (part * WIRE_SCALE).astype(jnp.float16)

    def decode(part):
        return part.astype(jnp.float32) * (1.0 / WIRE_SCALE)

    if number == 4:
        far_first = exchange(code(first), 2)
        coded_last = code(last)
        far = [exchange(coded_last, step) for step in (3, 2, 1)]
        first = first + decode(far_first)
        near = decode(exchange(code(first), 1))
        far = decode(far[0]) + decode(far[1]) + decode(far[2])
    else:
        first, last = lax.psum((first, last), "sta")
        near, far = jnp.zeros_like(first), jnp.zeros_like(last)
    return pl.pallas_call(
        functools.partial(finish, factor=math.sqrt(comps * taps)),
        out_shape=jax.ShapeDtypeStruct((count, samples), jnp.float32),
        in_specs=[vmem] * 4,
        out_specs=vmem,
        scratch_shapes=[pltpu.VMEM((count * rows, LANES), jnp.float32)],
        compiler_params=params,
        name="finish",
    )(first, near, last, far)


def solution(mesh):
    placed = (
        P(("grp", "sta"), None, "tm"),
        P(("grp", "sta"), "comp", None, None),
        P(("grp", "sta"), "comp"),
        P(("grp", "sta"), "tm"),
    )
    return jax.shard_map(
        shards, mesh=mesh, in_specs=placed, out_specs=P(("grp", "comp"), "tm"), check_vma=False
    )
```

```python
import functools
import math

import jax
import jax.numpy as jnp
from jax import lax
from jax.experimental import pallas as pl
from jax.experimental.pallas import tpu as pltpu
from jax.sharding import PartitionSpec as P

MOVE = 625

eps_energy = 1e-06
LANES = 128
GROUP = 16
COUNT_ROWS = 8
TILES = 4
WIRE_SCALE = 2.0**13


def from_next(value, axis):
    count = lax.axis_size(axis)
    arrived = lax.ppermute(value, axis, [(k, (k - 1) % count) for k in range(count)])
    return jnp.where(lax.axis_index(axis) == count - 1, jnp.zeros_like(arrived), arrived)


def turn_groups(rows):
    width = rows.shape[1]
    source = lax.broadcasted_iota(jnp.int32, (width, width), 0)
    target = lax.broadcasted_iota(jnp.int32, (width, width), 1)
    swap = jnp.where(source == (target // GROUP) * GROUP + (GROUP - 1 - target % GROUP), 1.0, 0.0)
    return jnp.dot(rows, swap.astype(rows.dtype), preferred_element_type=jnp.float32).astype(rows.dtype)


def prepare(bank_ref, turned_ref, scale_ref):
    stations, comps, count, taps = bank_ref.shape
    whole = taps // LANES
    tail = taps - whole * LANES
    chunks = []
    for s in range(stations):
        energy = None
        for c in range(comps):
            wide = bank_ref[s, c].astype(jnp.float32)
            term = jnp.sum(wide * wide, axis=1, keepdims=True)
            energy = term if energy is None else energy + term
            for q in range(whole):
                chunks.append(bank_ref[s, c, :, q * LANES : (q + 1) * LANES])
        scale_ref[s] = jnp.broadcast_to(lax.rsqrt(energy + eps_energy), (count, LANES))
    turned = turn_groups(jnp.concatenate(chunks, axis=0))
    for s in range(stations):
        for n in range(comps * whole):
            first = (s * comps * whole + n) * count
            turned_ref[s, :, n * LANES : (n + 1) * LANES] = turned[first : first + count]
        for c in range(comps):
            left = comps * whole * LANES + c * tail
            turned_ref[s, :, left : left + tail] = turn_groups(bank_ref[s, c, :, whole * LANES :])


def fill_hankel(window, hankel, stations, comps):
    for s in range(stations):
        for c in range(comps):
            line = window(s, c)
            width = line.shape[1]
            base = jnp.broadcast_to(line, (GROUP, width))
            for g in range(LANES // GROUP):
                amount = (width - GROUP * g - (GROUP - 1)) % width
                top = (s * comps + c) * LANES + GROUP * g
                hankel[top : top + GROUP, :] = pltpu.roll(base, amount, 1, stride=1, stride_axis=0)


def window_energy(square, taps):
    width = square.shape[1]
    sums, size = {1: square}, 1
    while 2 * size <= taps:
        sums[2 * size] = sums[size] + pltpu.roll(sums[size], width - size, 1)
        size *= 2
    energy, start = None, 0
    for size in sorted(sums, reverse=True):
        if start + size <= taps:
            piece = sums[size] if start == 0 else pltpu.roll(sums[size], width - start, 1)
            energy = piece if energy is None else energy + piece
            start += size
    return energy


def inverse_energy(square, taps):
    energy = window_energy(square, taps)
    return jnp.where(energy > 0.0, lax.rsqrt(energy + eps_energy), 0.0)


def products(inverse, turned_ref, scale_ref, hankel, taps, comps, tiles, put):
    stations, count, depth = turned_ref.shape
    whole = taps // LANES
    tail = taps - whole * LANES
    for s in range(stations):
        tops = [(s * comps + c) * LANES for c in range(comps)]
        for first in range(0, tiles, TILES):
            size = min(TILES, tiles - first)

            def part(top, rows, q):
                return hankel[top : top + rows, (first + q) * LANES : (first + q + size) * LANES]

            pieces = [part(top, LANES, q) for top in tops for q in range(whole)]
            pieces += [part(top, tail, whole) for top in tops]
            product = jnp.dot(turned_ref[s], jnp.concatenate(pieces, axis=0), preferred_element_type=jnp.float32)
            product = product * inverse[s : s + 1, first * LANES : (first + size) * LANES]
            for x in range(size):
                for g in range(0, count, 8):
                    tile = product[g : g + 8, x * LANES : (x + 1) * LANES] * scale_ref[s, g : g + 8, :]
                    put(s * count + g, first + x, tile)


def align(moves, flags, block, aligned, out_ref, rows):
    stations, count = moves.shape
    pitch = aligned.shape[0] // (stations * count)
    lane = lax.broadcasted_iota(jnp.int32, (rows, LANES), 1)
    for t in range(count):
        total = None
        for s in range(stations):
            move = moves[s, t]
            high = lax.shift_right_logical(move, 7)
            low = lax.bitwise_and(move, LANES - 1)
            at = (s * count + t) * pitch + high
            merged = jnp.where(lane >= low, aligned[pl.ds(at, rows), :], aligned[pl.ds(at + 1, rows), :])
            term = flags[s, block].astype(jnp.float32) * pltpu.roll(merged, LANES - low, 1)
            total = term if total is None else total + term
        out_ref[t * rows : (t + 1) * rows, :] = total


def put_counts(flags, out_ref, top):
    lane = lax.broadcasted_iota(jnp.int32, (COUNT_ROWS, LANES), 1)
    counts = jnp.zeros(lane.shape, jnp.float32)
    for b in range(flags.shape[1]):
        live = sum(flags[s, b] for s in range(flags.shape[0])).astype(jnp.float32)
        counts = jnp.where(lane == b, live, counts)
    out_ref[top : top + COUNT_ROWS, :] = counts


def by_part(source, target):
    stations, comps = target.shape[:2]
    return tuple((source.at[s, c], target.at[s, c]) for s in range(stations) for c in range(comps))


def fetch(pairs, ready):
    copies = [pltpu.make_async_copy(source, target, ready.at[n]) for n, (source, target) in enumerate(pairs)]
    for copy in copies:
        copy.start()
    return copies


def first_block(
    moves_hbm, flags_hbm, wave_hbm, bank_hbm, out_ref, later_ref, turned_ref, scale_ref, kept_ref,
    wave_ref, bank_ref, moves, flags, hankel, aligned, ready,
):
    comps, stations, samples = wave_ref.shape
    count, taps = bank_ref.shape[2:]
    rows = (out_ref.shape[0] - COUNT_ROWS) // count
    length = rows * LANES
    pitch = aligned.shape[0] // (stations * count)
    kept = kept_ref.shape[0] // (stations * count)
    copies = fetch((*by_part(bank_hbm, bank_ref), (wave_hbm, wave_ref), (moves_hbm, moves), (flags_hbm, flags)), ready)
    for copy in copies:
        copy.wait()
    put_counts(flags, out_ref, count * rows)
    later_ref[...] = wave_ref[:, :, samples - later_ref.shape[2] :]

    def window(s, c):
        return wave_ref[c, s : s + 1, : 2 * length]

    fill_hankel(window, hankel, stations, comps)
    wide = wave_ref[:, :, : 2 * length].astype(jnp.float32)
    inverse = inverse_energy(jnp.sum(wide * wide, axis=0), taps)
    prepare(bank_ref, turned_ref, scale_ref)

    def put(first, x, tile):
        aligned[pl.ds(first * pitch + x, 8, stride=pitch), :] = tile
        if rows <= x < rows + kept:
            kept_ref[pl.ds(first * kept + x - rows, 8, stride=kept), :] = tile

    products(inverse, turned_ref, scale_ref, hankel, taps, comps, pitch, put)
    align(moves, flags, 0, aligned, out_ref, rows)


def last_block(
    moves_hbm, flags_hbm, later_ref, next_ref, turned_ref, scale_ref, kept_ref, out_ref,
    moves, flags, hankel, aligned, ready, *, taps,
):
    comps, stations, own = later_ref.shape
    count = scale_ref.shape[1]
    rows = out_ref.shape[0] // count
    length = rows * LANES
    pitch = aligned.shape[0] // (stations * count)
    kept = kept_ref.shape[0] // (stations * count)
    copies = fetch(((moves_hbm, moves), (flags_hbm, flags)), ready)

    def window(s, c):
        return jnp.concatenate([later_ref[c, s : s + 1, :], next_ref[c, s : s + 1, :length]], axis=1)

    fill_hankel(window, hankel, stations, comps)
    squares = [jnp.sum(part * part, axis=0) for part in (later_ref[...].astype(jnp.float32), next_ref[:, :, :length].astype(jnp.float32))]
    inverse = inverse_energy(jnp.concatenate(squares, axis=1), taps)
    for first in range(0, stations * count, 8):
        for x in range(kept):
            aligned[pl.ds(first * pitch + x, 8, stride=pitch), :] = kept_ref[pl.ds(first * kept + x, 8, stride=kept), :]

    def put(first, x, tile):
        aligned[pl.ds(first * pitch + kept + x, 8, stride=pitch), :] = tile

    products(inverse, turned_ref, scale_ref, hankel, taps, comps, pitch - kept, put)
    for copy in copies:
        copy.wait()
    align(moves, flags, flags.shape[1] - 1, aligned, out_ref, rows)


def finish(first_ref, near_ref, last_ref, far_ref, out_ref, sums, *, factor):
    count, samples = out_ref.shape
    size = last_ref.shape[0]
    rows = size // count
    counts = first_ref[size:, :] + near_ref[size:, :]
    lane = lax.broadcasted_iota(jnp.int32, counts.shape, 1)
    for b, (own_ref, other_ref) in enumerate(((first_ref, near_ref), (last_ref, far_ref))):
        live = jnp.sum(jnp.where(lane == b, counts, 0.0), axis=1, keepdims=True)
        gain = jnp.broadcast_to(factor * lax.rsqrt(live), (COUNT_ROWS, LANES))
        for top in range(0, size, COUNT_ROWS):
            part = slice(top, top + COUNT_ROWS)
            sums[part, :] = (own_ref[part, :] + other_ref[part, :]) * gain
        for x in range(rows):
            left = (b * rows + x) * LANES
            for g in range(0, count, 8):
                out_ref[g : g + 8, left : left + LANES] = sums[pl.ds(g * rows + x, 8, stride=rows), :]


def in_hbm(value):
    return pltpu.with_memory_space_constraint(value, pltpu.HBM)


def shards(data, templates, moveouts, mask):
    stations, comps, samples = data.shape
    count, taps = templates.shape[1], templates.shape[3]
    blocks = mask.shape[1]
    length = samples // blocks
    assert blocks == 2 and length >= taps + MOVE - 1
    wave_own = jnp.transpose(data, (1, 0, 2))
    wave = pltpu.with_memory_space_constraint(wave_own, pltpu.HBM)
    bank = pltpu.with_memory_space_constraint(jnp.transpose(templates, (0, 2, 1, 3)), pltpu.HBM)
    following = from_next(wave_own, "tm")

    rows = length // LANES
    pitch = rows + -(-(MOVE - 1) // LANES)
    kept = (2 * length - taps + 1) // LANES - rows
    vmem = pl.BlockSpec(memory_space=pltpu.VMEM)
    hbm = pl.BlockSpec(memory_space=pl.ANY)
    last_width = 2 * length - kept * LANES

    def scratch(width):
        return [
            pltpu.SMEM(moveouts.shape, moveouts.dtype),
            pltpu.SMEM(mask.shape, mask.dtype),
            pltpu.VMEM((stations * comps * LANES, width), jnp.bfloat16),
            pltpu.VMEM((stations * count * pitch, LANES), jnp.float32),
        ]

    params = pltpu.CompilerParams(vmem_limit_bytes=32 * 2**20)
    first, later, turned, scale, both = pl.pallas_call(
        first_block,
        out_shape=(
            jax.ShapeDtypeStruct((count * rows + COUNT_ROWS, LANES), jnp.float32),
            jax.ShapeDtypeStruct((comps, stations, last_width - length), jnp.bfloat16),
            jax.ShapeDtypeStruct((stations, count, comps * taps), jnp.bfloat16),
            jax.ShapeDtypeStruct((stations, count, LANES), jnp.float32),
            jax.ShapeDtypeStruct((stations * count * kept, LANES), jnp.float32),
        ),
        in_specs=[hbm] * 4,
        out_specs=(vmem, vmem, vmem, vmem, vmem),
        scratch_shapes=[pltpu.VMEM(wave.shape, wave.dtype), pltpu.VMEM(bank.shape, bank.dtype)]
        + scratch(2 * length)
        + [pltpu.SemaphoreType.DMA((stations * comps + 3,))],
        compiler_params=params,
        name="first_block",
    )(in_hbm(moveouts), in_hbm(mask), wave, bank)
    last = pl.pallas_call(
        functools.partial(last_block, taps=taps),
        out_shape=jax.ShapeDtypeStruct((count * rows, LANES), jnp.float32),
        in_specs=[hbm] * 2 + [vmem] * 5,
        out_specs=vmem,
        scratch_shapes=scratch(last_width) + [pltpu.SemaphoreType.DMA((2,))],
        compiler_params=params,
        name="last_block",
    )(in_hbm(moveouts), in_hbm(mask), later, following, turned, scale, both)

    number = lax.axis_size("sta")

    def exchange(part, step):
        return lax.ppermute(part, "sta", [(k, k ^ step) for k in range(number)])

    def code(part):
        return (part * WIRE_SCALE).astype(jnp.float16)

    def decode(part):
        return part.astype(jnp.float32) * (1.0 / WIRE_SCALE)

    if number == 4:
        far_first = exchange(code(first), 2)
        coded_last = code(last)
        far = [exchange(coded_last, step) for step in (2, 1, 3)]
        first = first + decode(far_first)
        near = decode(exchange(code(first), 1))
        far = decode(far[0]) + decode(far[1]) + decode(far[2])
    else:
        first, last = lax.psum((first, last), "sta")
        near, far = jnp.zeros_like(first), jnp.zeros_like(last)
    return pl.pallas_call(
        functools.partial(finish, factor=math.sqrt(comps * taps)),
        out_shape=jax.ShapeDtypeStruct((count, samples), jnp.float32),
        in_specs=[vmem] * 4,
        out_specs=vmem,
        scratch_shapes=[pltpu.VMEM((count * rows, LANES), jnp.float32)],
        compiler_params=params,
        name="finish",
    )(first, near, last, far)


def solution(mesh):
    placed = (
        P(("grp", "sta"), None, "tm"),
        P(("grp", "sta"), "comp", None, None),
        P(("grp", "sta"), "comp"),
        P(("grp", "sta"), "tm"),
    )
    return jax.shard_map(
        shards, mesh=mesh, in_specs=placed, out_specs=P(("grp", "comp"), "tm"), check_vma=False
    )
```

```python
import functools
import math

import jax
import jax.numpy as jnp
from jax import lax
from jax.experimental import pallas as pl
from jax.experimental.pallas import tpu as pltpu
from jax.sharding import PartitionSpec as P

MOVE = 625

eps_energy = 1e-06
LANES = 128
GROUP = 16
COUNT_ROWS = 8
TILES = 4
WIRE_SCALE = 2.0**13


def from_next(value, axis):
    count = lax.axis_size(axis)
    arrived = lax.ppermute(value, axis, [(k, (k - 1) % count) for k in range(count)])
    return arrived


def turn_groups(rows):
    width = rows.shape[1]
    source = lax.broadcasted_iota(jnp.int32, (width, width), 0)
    target = lax.broadcasted_iota(jnp.int32, (width, width), 1)
    swap = jnp.where(source == (target // GROUP) * GROUP + (GROUP - 1 - target % GROUP), 1.0, 0.0)
    return jnp.dot(rows, swap.astype(rows.dtype), preferred_element_type=jnp.float32).astype(rows.dtype)


def prepare(bank_ref, turned_ref, scale_ref):
    stations, comps, count, taps = bank_ref.shape
    whole = taps // LANES
    tail = taps - whole * LANES
    chunks = []
    for s in range(stations):
        energy = None
        for c in range(comps):
            wide = bank_ref[s, c].astype(jnp.float32)
            term = jnp.sum(wide * wide, axis=1, keepdims=True)
            energy = term if energy is None else energy + term
            for q in range(whole):
                chunks.append(bank_ref[s, c, :, q * LANES : (q + 1) * LANES])
        scale_ref[s] = jnp.broadcast_to(lax.rsqrt(energy + eps_energy), (count, LANES))
    turned = turn_groups(jnp.concatenate(chunks, axis=0))
    for s in range(stations):
        for n in range(comps * whole):
            first = (s * comps * whole + n) * count
            turned_ref[s, :, n * LANES : (n + 1) * LANES] = turned[first : first + count]
        for c in range(comps):
            left = comps * whole * LANES + c * tail
            turned_ref[s, :, left : left + tail] = turn_groups(bank_ref[s, c, :, whole * LANES :])


def fill_hankel(window, hankel, stations, comps):
    for s in range(stations):
        for c in range(comps):
            line = window(s, c)
            width = line.shape[1]
            base = jnp.broadcast_to(line, (GROUP, width))
            for g in range(LANES // GROUP):
                amount = (width - GROUP * g - (GROUP - 1)) % width
                top = (s * comps + c) * LANES + GROUP * g
                hankel[top : top + GROUP, :] = pltpu.roll(base, amount, 1, stride=1, stride_axis=0)


def window_energy(square, taps):
    width = square.shape[1]
    sums, size = {1: square}, 1
    while 2 * size <= taps:
        sums[2 * size] = sums[size] + pltpu.roll(sums[size], width - size, 1)
        size *= 2
    energy, start = None, 0
    for size in sorted(sums, reverse=True):
        if start + size <= taps:
            piece = sums[size] if start == 0 else pltpu.roll(sums[size], width - start, 1)
            energy = piece if energy is None else energy + piece
            start += size
    return energy


def inverse_energy(square, taps):
    energy = window_energy(square, taps)
    return jnp.where(energy > 0.0, lax.rsqrt(energy + eps_energy), 0.0)


def products(inverse, turned_ref, scale_ref, hankel, taps, comps, tiles, put):
    stations, count, depth = turned_ref.shape
    whole = taps // LANES
    tail = taps - whole * LANES
    for s in range(stations):
        tops = [(s * comps + c) * LANES for c in range(comps)]
        for first in range(0, tiles, TILES):
            size = min(TILES, tiles - first)

            def part(top, rows, q):
                return hankel[top : top + rows, (first + q) * LANES : (first + q + size) * LANES]

            pieces = [part(top, LANES, q) for top in tops for q in range(whole)]
            pieces += [part(top, tail, whole) for top in tops]
            product = jnp.dot(turned_ref[s], jnp.concatenate(pieces, axis=0), preferred_element_type=jnp.float32)
            product = product * inverse[s : s + 1, first * LANES : (first + size) * LANES]
            for x in range(size):
                for g in range(0, count, 8):
                    tile = product[g : g + 8, x * LANES : (x + 1) * LANES] * scale_ref[s, g : g + 8, :]
                    put(s * count + g, first + x, tile)


def align(moves, flags, block, aligned, out_ref, rows):
    stations, count = moves.shape
    pitch = aligned.shape[0] // (stations * count)
    lane = lax.broadcasted_iota(jnp.int32, (rows, LANES), 1)
    for t in range(count):
        total = None
        for s in range(stations):
            move = moves[s, t]
            high = lax.shift_right_logical(move, 7)
            low = lax.bitwise_and(move, LANES - 1)
            at = (s * count + t) * pitch + high
            merged = jnp.where(lane >= low, aligned[pl.ds(at, rows), :], aligned[pl.ds(at + 1, rows), :])
            term = flags[s, block].astype(jnp.float32) * pltpu.roll(merged, LANES - low, 1)
            total = term if total is None else total + term
        out_ref[t * rows : (t + 1) * rows, :] = total


def put_counts(flags, out_ref, top):
    lane = lax.broadcasted_iota(jnp.int32, (COUNT_ROWS, LANES), 1)
    counts = jnp.zeros(lane.shape, jnp.float32)
    for b in range(flags.shape[1]):
        live = sum(flags[s, b] for s in range(flags.shape[0])).astype(jnp.float32)
        counts = jnp.where(lane == b, live, counts)
    out_ref[top : top + COUNT_ROWS, :] = counts


def by_part(source, target):
    stations, comps = target.shape[:2]
    return tuple((source.at[s, c], target.at[s, c]) for s in range(stations) for c in range(comps))


def fetch(pairs, ready):
    copies = [pltpu.make_async_copy(source, target, ready.at[n]) for n, (source, target) in enumerate(pairs)]
    for copy in copies:
        copy.start()
    return copies


def first_block(
    moves_hbm, flags_hbm, wave_hbm, bank_hbm, out_ref, later_ref, turned_ref, scale_ref, kept_ref,
    wave_ref, bank_ref, moves, flags, hankel, aligned, ready,
):
    comps, stations, samples = wave_ref.shape
    count, taps = bank_ref.shape[2:]
    rows = (out_ref.shape[0] - COUNT_ROWS) // count
    length = rows * LANES
    pitch = aligned.shape[0] // (stations * count)
    kept = kept_ref.shape[0] // (stations * count)
    copies = fetch((*by_part(bank_hbm, bank_ref), (wave_hbm, wave_ref), (moves_hbm, moves), (flags_hbm, flags)), ready)
    for copy in copies:
        copy.wait()
    put_counts(flags, out_ref, count * rows)
    later_ref[...] = wave_ref[:, :, samples - later_ref.shape[2] :]

    def window(s, c):
        return wave_ref[c, s : s + 1, : 2 * length]

    fill_hankel(window, hankel, stations, comps)
    wide = wave_ref[:, :, : 2 * length].astype(jnp.float32)
    inverse = inverse_energy(jnp.sum(wide * wide, axis=0), taps)
    prepare(bank_ref, turned_ref, scale_ref)

    def put(first, x, tile):
        aligned[pl.ds(first * pitch + x, 8, stride=pitch), :] = tile
        if rows <= x < rows + kept:
            kept_ref[pl.ds(first * kept + x - rows, 8, stride=kept), :] = tile

    products(inverse, turned_ref, scale_ref, hankel, taps, comps, pitch, put)
    align(moves, flags, 0, aligned, out_ref, rows)


def last_block(
    moves_hbm, flags_hbm, later_ref, next_ref, turned_ref, scale_ref, kept_ref, out_ref,
    moves, flags, hankel, aligned, ready, *, taps,
):
    comps, stations, own = later_ref.shape
    count = scale_ref.shape[1]
    rows = out_ref.shape[0] // count
    length = rows * LANES
    pitch = aligned.shape[0] // (stations * count)
    kept = kept_ref.shape[0] // (stations * count)
    copies = fetch(((moves_hbm, moves), (flags_hbm, flags)), ready)
    inside = jnp.where(lax.axis_index("tm") < lax.axis_size("tm") - 1, 1.0, 0.0).astype(next_ref.dtype)

    def after(c, s):
        return next_ref[c, s : s + 1, :length] * inside

    def window(s, c):
        return jnp.concatenate([later_ref[c, s : s + 1, :], after(c, s)], axis=1)

    fill_hankel(window, hankel, stations, comps)
    squares = [jnp.sum(part * part, axis=0) for part in (later_ref[...].astype(jnp.float32), (next_ref[:, :, :length] * inside).astype(jnp.float32))]
    inverse = inverse_energy(jnp.concatenate(squares, axis=1), taps)
    for first in range(0, stations * count, 8):
        for x in range(kept):
            aligned[pl.ds(first * pitch + x, 8, stride=pitch), :] = kept_ref[pl.ds(first * kept + x, 8, stride=kept), :]

    def put(first, x, tile):
        aligned[pl.ds(first * pitch + kept + x, 8, stride=pitch), :] = tile

    products(inverse, turned_ref, scale_ref, hankel, taps, comps, pitch - kept, put)
    for copy in copies:
        copy.wait()
    align(moves, flags, flags.shape[1] - 1, aligned, out_ref, rows)


def finish(first_ref, near_ref, last_ref, far_ref, out_ref, sums, *, factor):
    count, samples = out_ref.shape
    size = last_ref.shape[0]
    rows = size // count
    counts = first_ref[size:, :] + near_ref[size:, :]
    lane = lax.broadcasted_iota(jnp.int32, counts.shape, 1)
    for b, (own_ref, other_ref) in enumerate(((first_ref, near_ref), (last_ref, far_ref))):
        live = jnp.sum(jnp.where(lane == b, counts, 0.0), axis=1, keepdims=True)
        gain = jnp.broadcast_to(factor * lax.rsqrt(live), (COUNT_ROWS, LANES))
        for top in range(0, size, COUNT_ROWS):
            part = slice(top, top + COUNT_ROWS)
            sums[part, :] = (own_ref[part, :] + other_ref[part, :]) * gain
        for x in range(rows):
            left = (b * rows + x) * LANES
            for g in range(0, count, 8):
                out_ref[g : g + 8, left : left + LANES] = sums[pl.ds(g * rows + x, 8, stride=rows), :]


def in_hbm(value):
    return pltpu.with_memory_space_constraint(value, pltpu.HBM)


def shards(data, templates, moveouts, mask):
    stations, comps, samples = data.shape
    count, taps = templates.shape[1], templates.shape[3]
    blocks = mask.shape[1]
    length = samples // blocks
    assert blocks == 2 and length >= taps + MOVE - 1
    wave_own = jnp.transpose(data, (1, 0, 2))
    wave = pltpu.with_memory_space_constraint(wave_own, pltpu.HBM)
    bank = pltpu.with_memory_space_constraint(jnp.transpose(templates, (0, 2, 1, 3)), pltpu.HBM)
    following = from_next(wave_own, "tm")

    rows = length // LANES
    pitch = rows + -(-(MOVE - 1) // LANES)
    kept = (2 * length - taps + 1) // LANES - rows
    vmem = pl.BlockSpec(memory_space=pltpu.VMEM)
    hbm = pl.BlockSpec(memory_space=pl.ANY)
    last_width = 2 * length - kept * LANES

    def scratch(width):
        return [
            pltpu.SMEM(moveouts.shape, moveouts.dtype),
            pltpu.SMEM(mask.shape, mask.dtype),
            pltpu.VMEM((stations * comps * LANES, width), jnp.bfloat16),
            pltpu.VMEM((stations * count * pitch, LANES), jnp.float32),
        ]

    params = pltpu.CompilerParams(vmem_limit_bytes=32 * 2**20)
    first, later, turned, scale, both = pl.pallas_call(
        first_block,
        out_shape=(
            jax.ShapeDtypeStruct((count * rows + COUNT_ROWS, LANES), jnp.float32),
            jax.ShapeDtypeStruct((comps, stations, last_width - length), jnp.bfloat16),
            jax.ShapeDtypeStruct((stations, count, comps * taps), jnp.bfloat16),
            jax.ShapeDtypeStruct((stations, count, LANES), jnp.float32),
            jax.ShapeDtypeStruct((stations * count * kept, LANES), jnp.float32),
        ),
        in_specs=[hbm] * 4,
        out_specs=(vmem, vmem, vmem, vmem, vmem),
        scratch_shapes=[pltpu.VMEM(wave.shape, wave.dtype), pltpu.VMEM(bank.shape, bank.dtype)]
        + scratch(2 * length)
        + [pltpu.SemaphoreType.DMA((stations * comps + 3,))],
        compiler_params=params,
        name="first_block",
    )(in_hbm(moveouts), in_hbm(mask), wave, bank)
    last = pl.pallas_call(
        functools.partial(last_block, taps=taps),
        out_shape=jax.ShapeDtypeStruct((count * rows, LANES), jnp.float32),
        in_specs=[hbm] * 2 + [vmem] * 5,
        out_specs=vmem,
        scratch_shapes=scratch(last_width) + [pltpu.SemaphoreType.DMA((2,))],
        compiler_params=params,
        name="last_block",
    )(in_hbm(moveouts), in_hbm(mask), later, following, turned, scale, both)

    number = lax.axis_size("sta")

    def exchange(part, step):
        return lax.ppermute(part, "sta", [(k, k ^ step) for k in range(number)])

    def code(part):
        return (part * WIRE_SCALE).astype(jnp.float16)

    def decode(part):
        return part.astype(jnp.float32) * (1.0 / WIRE_SCALE)

    if number == 4:
        far_first = exchange(code(first), 2)
        coded_last = code(last)
        far = [exchange(coded_last, step) for step in (2, 1, 3)]
        first = first + decode(far_first)
        near = decode(exchange(code(first), 1))
        far = decode(far[0]) + decode(far[1]) + decode(far[2])
    else:
        first, last = lax.psum((first, last), "sta")
        near, far = jnp.zeros_like(first), jnp.zeros_like(last)
    return pl.pallas_call(
        functools.partial(finish, factor=math.sqrt(comps * taps)),
        out_shape=jax.ShapeDtypeStruct((count, samples), jnp.float32),
        in_specs=[vmem] * 4,
        out_specs=vmem,
        scratch_shapes=[pltpu.VMEM((count * rows, LANES), jnp.float32)],
        compiler_params=params,
        name="finish",
    )(first, near, last, far)


def solution(mesh):
    placed = (
        P(("grp", "sta"), None, "tm"),
        P(("grp", "sta"), "comp", None, None),
        P(("grp", "sta"), "comp"),
        P(("grp", "sta"), "tm"),
    )
    return jax.shard_map(
        shards, mesh=mesh, in_specs=placed, out_specs=P(("grp", "comp"), "tm"), check_vma=False
    )
```

```python
import functools
import math

import jax
import jax.numpy as jnp
from jax import lax
from jax.experimental import pallas as pl
from jax.experimental.pallas import tpu as pltpu
from jax.sharding import PartitionSpec as P

MOVE = 625

eps_energy = 1e-06
LANES = 128
GROUP = 16
COUNT_ROWS = 8
TILES = 3
WIRE_SCALE = 2.0**13


def from_next(value, axis):
    count = lax.axis_size(axis)
    arrived = lax.ppermute(value, axis, [(k, (k - 1) % count) for k in range(count)])
    return arrived


def turn_groups(rows):
    width = rows.shape[1]
    source = lax.broadcasted_iota(jnp.int32, (width, width), 0)
    target = lax.broadcasted_iota(jnp.int32, (width, width), 1)
    swap = jnp.where(source == (target // GROUP) * GROUP + (GROUP - 1 - target % GROUP), 1.0, 0.0)
    return jnp.dot(rows, swap.astype(rows.dtype), preferred_element_type=jnp.float32).astype(rows.dtype)


def prepare(bank_ref, turned_ref, scale_ref):
    stations, comps, count, taps = bank_ref.shape
    whole = taps // LANES
    tail = taps - whole * LANES
    chunks = []
    for s in range(stations):
        energy = None
        for c in range(comps):
            wide = bank_ref[s, c].astype(jnp.float32)
            term = jnp.sum(wide * wide, axis=1, keepdims=True)
            energy = term if energy is None else energy + term
            for q in range(whole):
                chunks.append(bank_ref[s, c, :, q * LANES : (q + 1) * LANES])
        scale_ref[s] = jnp.broadcast_to(lax.rsqrt(energy + eps_energy), (count, LANES))
    turned = turn_groups(jnp.concatenate(chunks, axis=0))
    for s in range(stations):
        for n in range(comps * whole):
            first = (s * comps * whole + n) * count
            turned_ref[s, :, n * LANES : (n + 1) * LANES] = turned[first : first + count]
        for c in range(comps):
            left = comps * whole * LANES + c * tail
            turned_ref[s, :, left : left + tail] = turn_groups(bank_ref[s, c, :, whole * LANES :])


def fill_hankel(window, hankel, stations, comps):
    for s in range(stations):
        for c in range(comps):
            line = window(s, c)
            width = line.shape[1]
            base = jnp.broadcast_to(line, (GROUP, width))
            for g in range(LANES // GROUP):
                amount = (width - GROUP * g - (GROUP - 1)) % width
                top = (s * comps + c) * LANES + GROUP * g
                hankel[top : top + GROUP, :] = pltpu.roll(base, amount, 1, stride=1, stride_axis=0)


def window_energy(square, taps):
    width = square.shape[1]
    sums, size = {1: square}, 1
    while 2 * size <= taps:
        sums[2 * size] = sums[size] + pltpu.roll(sums[size], width - size, 1)
        size *= 2
    energy, start = None, 0
    for size in sorted(sums, reverse=True):
        if start + size <= taps:
            piece = sums[size] if start == 0 else pltpu.roll(sums[size], width - start, 1)
            energy = piece if energy is None else energy + piece
            start += size
    return energy


def inverse_energy(square, taps):
    energy = window_energy(square, taps)
    return jnp.where(energy > 0.0, lax.rsqrt(energy + eps_energy), 0.0)


def products(inverse, turned_ref, scale_ref, hankel, taps, comps, tiles, put):
    stations, count, depth = turned_ref.shape
    whole = taps // LANES
    tail = taps - whole * LANES
    for s in range(stations):
        tops = [(s * comps + c) * LANES for c in range(comps)]
        for first in range(0, tiles, TILES):
            size = min(TILES, tiles - first)

            def part(top, rows, q):
                return hankel[top : top + rows, (first + q) * LANES : (first + q + size) * LANES]

            pieces = [part(top, LANES, q) for top in tops for q in range(whole)]
            pieces += [part(top, tail, whole) for top in tops]
            product = jnp.dot(turned_ref[s], jnp.concatenate(pieces, axis=0), preferred_element_type=jnp.float32)
            product = product * inverse[s : s + 1, first * LANES : (first + size) * LANES]
            for x in range(size):
                for g in range(0, count, 8):
                    tile = product[g : g + 8, x * LANES : (x + 1) * LANES] * scale_ref[s, g : g + 8, :]
                    put(s * count + g, first + x, tile)


def align(moves, flags, block, aligned, out_ref, rows):
    stations, count = moves.shape
    pitch = aligned.shape[0] // (stations * count)
    lane = lax.broadcasted_iota(jnp.int32, (rows, LANES), 1)
    for t in range(count):
        total = None
        for s in range(stations):
            move = moves[s, t]
            high = lax.shift_right_logical(move, 7)
            low = lax.bitwise_and(move, LANES - 1)
            at = (s * count + t) * pitch + high
            merged = jnp.where(lane >= low, aligned[pl.ds(at, rows), :], aligned[pl.ds(at + 1, rows), :])
            term = flags[s, block].astype(jnp.float32) * pltpu.roll(merged, LANES - low, 1)
            total = term if total is None else total + term
        out_ref[t * rows : (t + 1) * rows, :] = total


def put_counts(flags, out_ref, top):
    lane = lax.broadcasted_iota(jnp.int32, (COUNT_ROWS, LANES), 1)
    counts = jnp.zeros(lane.shape, jnp.float32)
    for b in range(flags.shape[1]):
        live = sum(flags[s, b] for s in range(flags.shape[0])).astype(jnp.float32)
        counts = jnp.where(lane == b, live, counts)
    out_ref[top : top + COUNT_ROWS, :] = counts


def by_part(source, target):
    stations, comps = target.shape[:2]
    return tuple((source.at[s, c], target.at[s, c]) for s in range(stations) for c in range(comps))


def fetch(pairs, ready):
    copies = [pltpu.make_async_copy(source, target, ready.at[n]) for n, (source, target) in enumerate(pairs)]
    for copy in copies:
        copy.start()
    return copies


def first_block(
    moves_hbm, flags_hbm, wave_hbm, bank_hbm, out_ref, later_ref, turned_ref, scale_ref, kept_ref,
    wave_ref, bank_ref, moves, flags, hankel, aligned, ready,
):
    comps, stations, samples = wave_ref.shape
    count, taps = bank_ref.shape[2:]
    rows = (out_ref.shape[0] - COUNT_ROWS) // count
    length = rows * LANES
    pitch = aligned.shape[0] // (stations * count)
    kept = kept_ref.shape[0] // (stations * count)
    copies = fetch((*by_part(bank_hbm, bank_ref), (wave_hbm, wave_ref), (moves_hbm, moves), (flags_hbm, flags)), ready)
    for copy in copies:
        copy.wait()
    put_counts(flags, out_ref, count * rows)
    later_ref[...] = wave_ref[:, :, samples - later_ref.shape[2] :]

    def window(s, c):
        return wave_ref[c, s : s + 1, : 2 * length]

    fill_hankel(window, hankel, stations, comps)
    wide = wave_ref[:, :, : 2 * length].astype(jnp.float32)
    inverse = inverse_energy(jnp.sum(wide * wide, axis=0), taps)
    prepare(bank_ref, turned_ref, scale_ref)

    def put(first, x, tile):
        aligned[pl.ds(first * pitch + x, 8, stride=pitch), :] = tile
        if rows <= x < rows + kept:
            kept_ref[pl.ds(first * kept + x - rows, 8, stride=kept), :] = tile

    products(inverse, turned_ref, scale_ref, hankel, taps, comps, pitch, put)
    align(moves, flags, 0, aligned, out_ref, rows)


def last_block(
    moves_hbm, flags_hbm, later_ref, next_ref, turned_ref, scale_ref, kept_ref, out_ref,
    moves, flags, hankel, aligned, ready, *, taps,
):
    comps, stations, own = later_ref.shape
    count = scale_ref.shape[1]
    rows = out_ref.shape[0] // count
    length = rows * LANES
    pitch = aligned.shape[0] // (stations * count)
    kept = kept_ref.shape[0] // (stations * count)
    copies = fetch(((moves_hbm, moves), (flags_hbm, flags)), ready)
    inside = jnp.where(lax.axis_index("tm") < lax.axis_size("tm") - 1, 1.0, 0.0).astype(next_ref.dtype)

    def after(c, s):
        return next_ref[c, s : s + 1, :length] * inside

    def window(s, c):
        return jnp.concatenate([later_ref[c, s : s + 1, :], after(c, s)], axis=1)

    fill_hankel(window, hankel, stations, comps)
    squares = [jnp.sum(part * part, axis=0) for part in (later_ref[...].astype(jnp.float32), (next_ref[:, :, :length] * inside).astype(jnp.float32))]
    inverse = inverse_energy(jnp.concatenate(squares, axis=1), taps)
    for first in range(0, stations * count, 8):
        for x in range(kept):
            aligned[pl.ds(first * pitch + x, 8, stride=pitch), :] = kept_ref[pl.ds(first * kept + x, 8, stride=kept), :]

    def put(first, x, tile):
        aligned[pl.ds(first * pitch + kept + x, 8, stride=pitch), :] = tile

    products(inverse, turned_ref, scale_ref, hankel, taps, comps, pitch - kept, put)
    for copy in copies:
        copy.wait()
    align(moves, flags, flags.shape[1] - 1, aligned, out_ref, rows)


def finish(first_ref, near_ref, last_ref, far_ref, out_ref, sums, *, factor):
    count, samples = out_ref.shape
    size = last_ref.shape[0]
    rows = size // count
    counts = first_ref[size:, :] + near_ref[size:, :]
    lane = lax.broadcasted_iota(jnp.int32, counts.shape, 1)
    for b, (own_ref, other_ref) in enumerate(((first_ref, near_ref), (last_ref, far_ref))):
        live = jnp.sum(jnp.where(lane == b, counts, 0.0), axis=1, keepdims=True)
        gain = jnp.broadcast_to(factor * lax.rsqrt(live), (COUNT_ROWS, LANES))
        for top in range(0, size, COUNT_ROWS):
            part = slice(top, top + COUNT_ROWS)
            sums[part, :] = (own_ref[part, :] + other_ref[part, :]) * gain
        for x in range(rows):
            left = (b * rows + x) * LANES
            for g in range(0, count, 8):
                out_ref[g : g + 8, left : left + LANES] = sums[pl.ds(g * rows + x, 8, stride=rows), :]


def in_hbm(value):
    return pltpu.with_memory_space_constraint(value, pltpu.HBM)


def shards(data, templates, moveouts, mask):
    stations, comps, samples = data.shape
    count, taps = templates.shape[1], templates.shape[3]
    blocks = mask.shape[1]
    length = samples // blocks
    assert blocks == 2 and length >= taps + MOVE - 1
    wave_own = jnp.transpose(data, (1, 0, 2))
    wave = pltpu.with_memory_space_constraint(wave_own, pltpu.HBM)
    bank = pltpu.with_memory_space_constraint(jnp.transpose(templates, (0, 2, 1, 3)), pltpu.HBM)
    following = from_next(wave_own, "tm")

    rows = length // LANES
    pitch = rows + -(-(MOVE - 1) // LANES)
    kept = (2 * length - taps + 1) // LANES - rows
    vmem = pl.BlockSpec(memory_space=pltpu.VMEM)
    hbm = pl.BlockSpec(memory_space=pl.ANY)
    last_width = 2 * length - kept * LANES

    def scratch(width):
        return [
            pltpu.SMEM(moveouts.shape, moveouts.dtype),
            pltpu.SMEM(mask.shape, mask.dtype),
            pltpu.VMEM((stations * comps * LANES, width), jnp.bfloat16),
            pltpu.VMEM((stations * count * pitch, LANES), jnp.float32),
        ]

    params = pltpu.CompilerParams(vmem_limit_bytes=32 * 2**20)
    first, later, turned, scale, both = pl.pallas_call(
        first_block,
        out_shape=(
            jax.ShapeDtypeStruct((count * rows + COUNT_ROWS, LANES), jnp.float32),
            jax.ShapeDtypeStruct((comps, stations, last_width - length), jnp.bfloat16),
            jax.ShapeDtypeStruct((stations, count, comps * taps), jnp.bfloat16),
            jax.ShapeDtypeStruct((stations, count, LANES), jnp.float32),
            jax.ShapeDtypeStruct((stations * count * kept, LANES), jnp.float32),
        ),
        in_specs=[hbm] * 4,
        out_specs=(vmem, vmem, vmem, vmem, vmem),
        scratch_shapes=[pltpu.VMEM(wave.shape, wave.dtype), pltpu.VMEM(bank.shape, bank.dtype)]
        + scratch(2 * length)
        + [pltpu.SemaphoreType.DMA((stations * comps + 3,))],
        compiler_params=params,
        name="first_block",
    )(in_hbm(moveouts), in_hbm(mask), wave, bank)
    last = pl.pallas_call(
        functools.partial(last_block, taps=taps),
        out_shape=jax.ShapeDtypeStruct((count * rows, LANES), jnp.float32),
        in_specs=[hbm] * 2 + [vmem] * 5,
        out_specs=vmem,
        scratch_shapes=scratch(last_width) + [pltpu.SemaphoreType.DMA((2,))],
        compiler_params=params,
        name="last_block",
    )(in_hbm(moveouts), in_hbm(mask), later, following, turned, scale, both)

    number = lax.axis_size("sta")

    def exchange(part, step):
        return lax.ppermute(part, "sta", [(k, k ^ step) for k in range(number)])

    def code(part):
        return (part * WIRE_SCALE).astype(jnp.float16)

    def decode(part):
        return part.astype(jnp.float32) * (1.0 / WIRE_SCALE)

    if number == 4:
        far_first = exchange(code(first), 2)
        coded_last = code(last)
        far = [exchange(coded_last, step) for step in (2, 1, 3)]
        first = first + decode(far_first)
        near = decode(exchange(code(first), 1))
        far = decode(far[0]) + decode(far[1]) + decode(far[2])
    else:
        first, last = lax.psum((first, last), "sta")
        near, far = jnp.zeros_like(first), jnp.zeros_like(last)
    return pl.pallas_call(
        functools.partial(finish, factor=math.sqrt(comps * taps)),
        out_shape=jax.ShapeDtypeStruct((count, samples), jnp.float32),
        in_specs=[vmem] * 4,
        out_specs=vmem,
        scratch_shapes=[pltpu.VMEM((count * rows, LANES), jnp.float32)],
        compiler_params=params,
        name="finish",
    )(first, near, last, far)


def solution(mesh):
    placed = (
        P(("grp", "sta"), None, "tm"),
        P(("grp", "sta"), "comp", None, None),
        P(("grp", "sta"), "comp"),
        P(("grp", "sta"), "tm"),
    )
    return jax.shard_map(
        shards, mesh=mesh, in_specs=placed, out_specs=P(("grp", "comp"), "tm"), check_vma=False
    )
```

```python
import functools
import math

import jax
import jax.numpy as jnp
from jax import lax
from jax.experimental import pallas as pl
from jax.experimental.pallas import tpu as pltpu
from jax.sharding import PartitionSpec as P

MOVE = 625

eps_energy = 1e-06
LANES = 128
GROUP = 16
COUNT_ROWS = 8
TILES = 4
WIRE_SCALE = 2.0**13


def from_next(value, axis):
    count = lax.axis_size(axis)
    arrived = lax.ppermute(value, axis, [(k, (k - 1) % count) for k in range(count)])
    return arrived


def turn_groups(rows):
    width = rows.shape[1]
    source = lax.broadcasted_iota(jnp.int32, (width, width), 0)
    target = lax.broadcasted_iota(jnp.int32, (width, width), 1)
    swap = jnp.where(source == (target // GROUP) * GROUP + (GROUP - 1 - target % GROUP), 1.0, 0.0)
    return jnp.dot(rows, swap.astype(rows.dtype), preferred_element_type=jnp.float32).astype(rows.dtype)


def prepare(bank_ref, turned_ref, scale_ref):
    stations, comps, count, taps = bank_ref.shape
    whole = taps // LANES
    tail = taps - whole * LANES
    chunks = []
    for s in range(stations):
        energy = None
        for c in range(comps):
            wide = bank_ref[s, c].astype(jnp.float32)
            term = jnp.sum(wide * wide, axis=1, keepdims=True)
            energy = term if energy is None else energy + term
            for q in range(whole):
                chunks.append(bank_ref[s, c, :, q * LANES : (q + 1) * LANES])
        scale_ref[s] = jnp.broadcast_to(lax.rsqrt(energy + eps_energy), (count, LANES))
    turned = turn_groups(jnp.concatenate(chunks, axis=0))
    for s in range(stations):
        for n in range(comps * whole):
            first = (s * comps * whole + n) * count
            turned_ref[s, :, n * LANES : (n + 1) * LANES] = turned[first : first + count]
        for c in range(comps):
            left = comps * whole * LANES + c * tail
            turned_ref[s, :, left : left + tail] = turn_groups(bank_ref[s, c, :, whole * LANES :])


def fill_hankel(window, hankel, stations, comps):
    for s in range(stations):
        for c in range(comps):
            line = window(s, c)
            width = line.shape[1]
            base = jnp.broadcast_to(line, (GROUP, width))
            for g in range(LANES // GROUP):
                amount = (width - GROUP * g - (GROUP - 1)) % width
                top = (s * comps + c) * LANES + GROUP * g
                hankel[top : top + GROUP, :] = pltpu.roll(base, amount, 1, stride=1, stride_axis=0)


def window_energy(square, taps):
    width = square.shape[1]
    sums, size = {1: square}, 1
    while 2 * size <= taps:
        sums[2 * size] = sums[size] + pltpu.roll(sums[size], width - size, 1)
        size *= 2
    energy, start = None, 0
    for size in sorted(sums, reverse=True):
        if start + size <= taps:
            piece = sums[size] if start == 0 else pltpu.roll(sums[size], width - start, 1)
            energy = piece if energy is None else energy + piece
            start += size
    return energy


def inverse_energy(square, taps):
    energy = window_energy(square, taps)
    return jnp.where(energy > 0.0, lax.rsqrt(energy + eps_energy), 0.0)


def products(inverse, turned_ref, scale_ref, hankel, taps, comps, tiles, put):
    stations, count, depth = turned_ref.shape
    whole = taps // LANES
    tail = taps - whole * LANES
    for s in range(stations):
        tops = [(s * comps + c) * LANES for c in range(comps)]
        for first in range(0, tiles, TILES):
            size = min(TILES, tiles - first)

            def part(top, rows, q):
                return hankel[top : top + rows, (first + q) * LANES : (first + q + size) * LANES]

            pieces = [part(top, LANES, q) for top in tops for q in range(whole)]
            pieces += [part(top, tail, whole) for top in tops]
            product = jnp.dot(turned_ref[s], jnp.concatenate(pieces, axis=0), preferred_element_type=jnp.float32)
            product = product * inverse[s : s + 1, first * LANES : (first + size) * LANES]
            for x in range(size):
                for g in range(0, count, 8):
                    tile = product[g : g + 8, x * LANES : (x + 1) * LANES] * scale_ref[s, g : g + 8, :]
                    put(s * count + g, first + x, tile)


def align(moves, flags, block, aligned, out_ref, rows):
    stations, count = moves.shape
    pitch = aligned.shape[0] // (stations * count)
    lane = lax.broadcasted_iota(jnp.int32, (rows, LANES), 1)
    for t in range(count):
        total = None
        for s in range(stations):
            move = moves[s, t]
            high = lax.shift_right_logical(move, 7)
            low = lax.bitwise_and(move, LANES - 1)
            at = (s * count + t) * pitch + high
            merged = jnp.where(lane >= low, aligned[pl.ds(at, rows), :], aligned[pl.ds(at + 1, rows), :])
            term = flags[s, block].astype(jnp.float32) * pltpu.roll(merged, LANES - low, 1)
            total = term if total is None else total + term
        out_ref[t * rows : (t + 1) * rows, :] = total


def put_counts(flags, out_ref, top):
    lane = lax.broadcasted_iota(jnp.int32, (COUNT_ROWS, LANES), 1)
    counts = jnp.zeros(lane.shape, jnp.float32)
    for b in range(flags.shape[1]):
        live = sum(flags[s, b] for s in range(flags.shape[0])).astype(jnp.float32)
        counts = jnp.where(lane == b, live, counts)
    out_ref[top : top + COUNT_ROWS, :] = counts


def by_part(source, target):
    stations, comps = target.shape[:2]
    return tuple((source.at[s, c], target.at[s, c]) for s in range(stations) for c in range(comps))


def fetch(pairs, ready):
    copies = [pltpu.make_async_copy(source, target, ready.at[n]) for n, (source, target) in enumerate(pairs)]
    for copy in copies:
        copy.start()
    return copies


def first_block(
    moves_hbm, flags_hbm, wave_hbm, bank_hbm, out_ref, later_ref, turned_ref, scale_ref, kept_ref,
    wave_ref, bank_ref, moves, flags, hankel, aligned, ready,
):
    comps, stations, samples = wave_ref.shape
    count, taps = bank_ref.shape[2:]
    rows = (out_ref.shape[0] - COUNT_ROWS) // count
    length = rows * LANES
    pitch = aligned.shape[0] // (stations * count)
    kept = kept_ref.shape[0] // (stations * count)
    copies = fetch((*by_part(bank_hbm, bank_ref), (wave_hbm, wave_ref), (moves_hbm, moves), (flags_hbm, flags)), ready)
    for copy in copies:
        copy.wait()
    put_counts(flags, out_ref, count * rows)
    later_ref[...] = wave_ref[:, :, samples - later_ref.shape[2] :]

    def window(s, c):
        return wave_ref[c, s : s + 1, : 2 * length]

    fill_hankel(window, hankel, stations, comps)
    wide = wave_ref[:, :, : 2 * length].astype(jnp.float32)
    inverse = inverse_energy(jnp.sum(wide * wide, axis=0), taps)
    prepare(bank_ref, turned_ref, scale_ref)

    def put(first, x, tile):
        aligned[pl.ds(first * pitch + x, 8, stride=pitch), :] = tile
        if rows <= x < rows + kept:
            kept_ref[pl.ds(first * kept + x - rows, 8, stride=kept), :] = tile

    products(inverse, turned_ref, scale_ref, hankel, taps, comps, pitch, put)
    align(moves, flags, 0, aligned, out_ref, rows)


def last_block(
    moves_hbm, flags_hbm, later_ref, next_ref, turned_ref, scale_ref, kept_ref, out_ref,
    moves, flags, hankel, aligned, ready, *, taps,
):
    comps, stations, own = later_ref.shape
    count = scale_ref.shape[1]
    rows = out_ref.shape[0] // count
    length = rows * LANES
    pitch = aligned.shape[0] // (stations * count)
    kept = kept_ref.shape[0] // (stations * count)
    copies = fetch(((moves_hbm, moves), (flags_hbm, flags)), ready)
    inside = jnp.where(lax.axis_index("tm") < lax.axis_size("tm") - 1, 1.0, 0.0).astype(next_ref.dtype)

    def after(c, s):
        return next_ref[c, s : s + 1, :length] * inside

    def window(s, c):
        return jnp.concatenate([later_ref[c, s : s + 1, :], after(c, s)], axis=1)

    fill_hankel(window, hankel, stations, comps)
    squares = [jnp.sum(part * part, axis=0) for part in (later_ref[...].astype(jnp.float32), (next_ref[:, :, :length] * inside).astype(jnp.float32))]
    inverse = inverse_energy(jnp.concatenate(squares, axis=1), taps)
    for first in range(0, stations * count, 8):
        for x in range(kept):
            aligned[pl.ds(first * pitch + x, 8, stride=pitch), :] = kept_ref[pl.ds(first * kept + x, 8, stride=kept), :]

    def put(first, x, tile):
        aligned[pl.ds(first * pitch + kept + x, 8, stride=pitch), :] = tile

    products(inverse, turned_ref, scale_ref, hankel, taps, comps, pitch - kept, put)
    for copy in copies:
        copy.wait()
    align(moves, flags, flags.shape[1] - 1, aligned, out_ref, rows)


def finish(first_ref, near_ref, last_ref, far_ref, out_ref, sums, *, factor):
    count, samples = out_ref.shape
    size = last_ref.shape[0]
    rows = size // count
    counts = first_ref[size:, :] + near_ref[size:, :]
    lane = lax.broadcasted_iota(jnp.int32, counts.shape, 1)
    for b, (own_ref, other_ref) in enumerate(((first_ref, near_ref), (last_ref, far_ref))):
        live = jnp.sum(jnp.where(lane == b, counts, 0.0), axis=1, keepdims=True)
        gain = jnp.broadcast_to(factor * lax.rsqrt(live), (COUNT_ROWS, LANES))
        for top in range(0, size, COUNT_ROWS):
            part = slice(top, top + COUNT_ROWS)
            sums[part, :] = (own_ref[part, :] + other_ref[part, :]) * gain
        for x in range(rows):
            left = (b * rows + x) * LANES
            for g in range(0, count, 8):
                out_ref[g : g + 8, left : left + LANES] = sums[pl.ds(g * rows + x, 8, stride=rows), :]


def in_hbm(value):
    return pltpu.with_memory_space_constraint(value, pltpu.HBM)


def shards(data, templates, moveouts, mask):
    stations, comps, samples = data.shape
    count, taps = templates.shape[1], templates.shape[3]
    blocks = mask.shape[1]
    length = samples // blocks
    assert blocks == 2 and length >= taps + MOVE - 1
    wave_own = jnp.transpose(data, (1, 0, 2))
    wave = pltpu.with_memory_space_constraint(wave_own, pltpu.HBM)
    bank = pltpu.with_memory_space_constraint(jnp.transpose(templates, (0, 2, 1, 3)), pltpu.HBM)
    following = from_next(wave_own, "tm")

    rows = length // LANES
    pitch = rows + -(-(MOVE - 1) // LANES)
    kept = (2 * length - taps + 1) // LANES - rows
    vmem = pl.BlockSpec(memory_space=pltpu.VMEM)
    hbm = pl.BlockSpec(memory_space=pl.ANY)
    last_width = 2 * length - kept * LANES

    def scratch(width):
        return [
            pltpu.SMEM(moveouts.shape, moveouts.dtype),
            pltpu.SMEM(mask.shape, mask.dtype),
            pltpu.VMEM((stations * comps * LANES, width), jnp.bfloat16),
            pltpu.VMEM((stations * count * pitch, LANES), jnp.float32),
        ]

    params = pltpu.CompilerParams(vmem_limit_bytes=32 * 2**20)
    first, later, turned, scale, both = pl.pallas_call(
        first_block,
        out_shape=(
            jax.ShapeDtypeStruct((count * rows + COUNT_ROWS, LANES), jnp.float32),
            jax.ShapeDtypeStruct((comps, stations, last_width - length), jnp.bfloat16),
            jax.ShapeDtypeStruct((stations, count, comps * taps), jnp.bfloat16),
            jax.ShapeDtypeStruct((stations, count, LANES), jnp.float32),
            jax.ShapeDtypeStruct((stations * count * kept, LANES), jnp.float32),
        ),
        in_specs=[hbm] * 4,
        out_specs=(vmem, vmem, vmem, vmem, vmem),
        scratch_shapes=[pltpu.VMEM(wave.shape, wave.dtype), pltpu.VMEM(bank.shape, bank.dtype)]
        + scratch(2 * length)
        + [pltpu.SemaphoreType.DMA((stations * comps + 3,))],
        compiler_params=params,
        name="first_block",
    )(in_hbm(moveouts), in_hbm(mask), wave, bank)
    last = pl.pallas_call(
        functools.partial(last_block, taps=taps),
        out_shape=jax.ShapeDtypeStruct((count * rows, LANES), jnp.float32),
        in_specs=[hbm] * 2 + [vmem] * 5,
        out_specs=vmem,
        scratch_shapes=scratch(last_width) + [pltpu.SemaphoreType.DMA((2,))],
        compiler_params=params,
        name="last_block",
    )(in_hbm(moveouts), in_hbm(mask), later, following, turned, scale, both)

    number = lax.axis_size("sta")

    def exchange(part, step):
        return lax.ppermute(part, "sta", [(k, k ^ step) for k in range(number)])

    def around(part, step):
        return lax.ppermute(part, "sta", [(k, (k + step) % number) for k in range(number)])

    def code(part):
        return (part * WIRE_SCALE).astype(jnp.float16)

    def decode(part):
        return part.astype(jnp.float32) * (1.0 / WIRE_SCALE)

    if number == 4:
        far_first = exchange(code(first), 2)
        coded_last = code(last)
        far = [around(coded_last, step) for step in (3, 1, 2)]
        first = first + decode(far_first)
        near = decode(exchange(code(first), 1))
        far = decode(far[0]) + decode(far[1]) + decode(far[2])
    else:
        first, last = lax.psum((first, last), "sta")
        near, far = jnp.zeros_like(first), jnp.zeros_like(last)
    return pl.pallas_call(
        functools.partial(finish, factor=math.sqrt(comps * taps)),
        out_shape=jax.ShapeDtypeStruct((count, samples), jnp.float32),
        in_specs=[vmem] * 4,
        out_specs=vmem,
        scratch_shapes=[pltpu.VMEM((count * rows, LANES), jnp.float32)],
        compiler_params=params,
        name="finish",
    )(first, near, last, far)


def solution(mesh):
    placed = (
        P(("grp", "sta"), None, "tm"),
        P(("grp", "sta"), "comp", None, None),
        P(("grp", "sta"), "comp"),
        P(("grp", "sta"), "tm"),
    )
    return jax.shard_map(
        shards, mesh=mesh, in_specs=placed, out_specs=P(("grp", "comp"), "tm"), check_vma=False
    )
```
